256 devices in a mesh: mer: 64 (over z, x, core), blk: 4 (over y).
Axes of the slice: x: 4, y: 4, z: 8, core: 2. Of those that a mesh axis runs over, the one named last changes fastest.
Arguments:
- disp_now: float32 [8000, 2, 2048], P('mer', None, 'blk'), may hold values from -6 to 6
- disp_prev: float32 [8000, 2, 2048], P('mer', None, 'blk'), may hold values from -6 to 6
- kappa: bfloat16 [8000, 4096], P('mer', 'blk'), may hold values from 0.5 to 4
- radius: float32 [8000], P('mer'), may hold values from 50 to 2000
- fwd_strain: bfloat16 [2, 3, 8000, 4096], P(None, None, 'mer', 'blk'), may hold values from -6 to 6
- order_bucket: int32 [320], P('mer'), may hold values from 0 to 3
- shared_nodes: int32 [64, 2, 5], P('mer'), may hold values from 0 to 124
- region_map: int32 [320], P('mer'), may hold values from 0 to 4095
Outputs:
- displacement: float32 [8000, 2, 2048], P('mer', None, 'blk')
- kernel: float32 [4096, 1024], P('mer', 'blk')
The draws below stay inside these ranges and needn't reach their ends.
Inputs may be any that keep to these rules, and one draw needn't show every extreme that they name: `shared_nodes`: entry k of row 1 of partition i and entry k of row 0 of partition i + 1 name the same physical node; row 0 of the first and row 1 of the last partition name no partner.
All inputs are finite; a program needn't handle non-finite values.
Results may differ from the reference program's by a relative error of at most 0.0031.
The reference program's roundings to bfloat16 on the way count: a program that leaves them out, or rounds other values in their place, can miss the bound.
Values may be sent and summed in bfloat16 or wider, within the bound.
No kernel may reach another device: no remote copies, remote signals or barrier semaphores. Data moves between devices by JAX's collectives and lax.ppermute only.
A program may use at most 128 MiB of HBM per device.

```python
import math
import jax
import jax.numpy as jnp
import numpy as np
from jax import lax

E_DEV = 5
MAXO = 2048
NSH = 5
STEPS = 2
ELEMS = 320
POINTS = 8000
NPHI = 4096
NREG = 4096
NSECT = 1024
N_MER = 64


def with_ends(values, key, least, top_value):
    shape = values.shape
    spot = [jax.random.randint(jax.random.fold_in(key, axis), (), 0, shape[axis]) for axis in range(len(shape))]
    values = values.at[tuple(spot)].set(least)
    longest = shape.index(max(shape))
    spot[longest] = (spot[longest] + 1) % shape[longest]
    return values.at[tuple(spot)].set(top_value)


def shard_levels(key, shape, pieces, smallest, top_value):
    loudness = 1.0
    for dim, shards_of in pieces:
        heights = jax.random.uniform(jax.random.fold_in(jax.random.fold_in(key, 6), dim), (shards_of,), jnp.float32, smallest / len(pieces), top_value / len(pieces))
        loudness = loudness * jnp.repeat(jnp.exp(heights), shape[dim] // shards_of).reshape((-1,) + (1,) * (len(shape) - 1 - dim))
    return loudness


def bell_draw(rng, extent, scale, most, pieces=(), kind=jnp.bfloat16):
    result = jax.random.normal(rng, extent, jnp.float32) * scale
    if len(pieces) > 0:
        result = shard_levels(rng, extent, pieces, -0.22, 0.18) * result
    return jnp.clip(result, min=-most, max=most).astype(kind)


def setup_inputs(seed: int = 0) -> dict:
    streams_of = jax.random.split(jax.random.key(seed), 9)
    disp_now = bell_draw(streams_of[0], (POINTS, 2, MAXO), 1.0, 6.0, ((0, 64), (2, 4)), jnp.float32)
    disp_prev = bell_draw(streams_of[1], (POINTS, 2, MAXO), 1.0, 6.0, ((0, 64), (2, 4)), jnp.float32)
    kappa = jnp.clip(jnp.exp(math.log(4.0) - 2.0794415 * jax.random.uniform(streams_of[2], (POINTS, NPHI), jnp.float32) ** shard_levels(streams_of[2], (POINTS, NPHI), ((0, 64), (1, 4)), -0.2, 0.2)), 0.5, 4.0).astype(jnp.bfloat16)
    radius = jnp.clip(jnp.exp(math.log(2000.0) - 3.6888795 * jax.random.uniform(streams_of[3], (POINTS,), jnp.float32) ** shard_levels(streams_of[3], (POINTS,), ((0, 64),), -0.2, 0.2)), 50.0, 2000.0)
    fwd_strain = bell_draw(streams_of[4], (STEPS, 3, POINTS, NPHI), 1.0, 6.0, ((2, 64), (3, 4)))
    order_bucket = with_ends(jax.random.randint(streams_of[5], (ELEMS,), 0, 4), jax.random.fold_in(streams_of[5], 1), 0, 3).astype(jnp.int32)
    shared_nodes = with_ends(jax.random.randint(streams_of[6], (N_MER, 2, NSH), 0, 25 * E_DEV), jax.random.fold_in(streams_of[6], 1), 0, (25 * E_DEV) - 1).astype(jnp.int32)
    region_map = with_ends(jax.random.randint(streams_of[7], (ELEMS,), 0, NREG), jax.random.fold_in(streams_of[7], 1), 0, NREG - 1).astype(jnp.int32)
    return dict(disp_now=disp_now, disp_prev=disp_prev, kappa=kappa, radius=radius, fwd_strain=fwd_strain, order_bucket=order_bucket, shared_nodes=shared_nodes, region_map=region_map)


time_step_sq = 0.0004
kernel_scale = 0.0001
bucket_orders = (8, 64, 512, 2048)

def gll_tables():
    nodes = np.array([-1.0, -math.sqrt(3.0 / 7.0), 0.0, math.sqrt(3.0 / 7.0), 1.0])
    weights_line = np.array([0.1, 49.0 / 90.0, 32.0 / 45.0, 49.0 / 90.0, 0.1])
    legendre = (35.0 * nodes ** 4 - 30.0 * nodes ** 2 + 3.0) / 8.0
    deriv = np.zeros((5, 5))
    for row_index in range(5):
        for col_index in range(5):
            if row_index != col_index:
                deriv[row_index, col_index] = legendre[row_index] / legendre[col_index] / (nodes[row_index] - nodes[col_index])
    deriv[0, 0] = -5.0
    deriv[4, 4] = 5.0
    return (deriv, np.outer(weights_line, weights_line).reshape(25))

def order_mask(bucket, orders):
    levels = jnp.zeros(bucket.shape, jnp.int32)
    for position, value in enumerate(bucket_orders):
        levels = levels + jnp.where(bucket == position, value, 0).astype(jnp.int32)
    levels = jnp.repeat(levels, 25)
    cosine_part = orders[None, :] < levels[:, None]
    sine_part = cosine_part & (orders[None, :] >= 1)
    return jnp.stack([cosine_part, sine_part], axis=1).astype(jnp.float32)

def fourier_table(orders, samples, nphi):
    turns = orders[:, None] * samples[None, :] % nphi
    angle = turns.astype(jnp.float32) * (2.0 * math.pi / nphi)
    return jnp.stack([jnp.cos(angle), jnp.sin(angle)]).astype(jnp.bfloat16)

def strains(field, radius, orders, deriv):
    points, parts, count = field.shape
    shaped = field.reshape(points // 25, 5, 5, parts, count)
    along_s = jnp.einsum('aj,ejbcm->eabcm', deriv, shaped, precision=lax.Precision.HIGHEST).reshape(field.shape)
    along_z = jnp.einsum('bj,eajcm->eabcm', deriv, shaped, precision=lax.Precision.HIGHEST).reshape(field.shape)
    scale = orders.astype(jnp.float32)[None, :] / radius[:, None]
    beside_all = jnp.stack([scale * field[:, 1], -scale * field[:, 0]], axis=1)
    return jnp.stack([along_s, along_z, beside_all])

def divergence(back, radius, orders, deriv):
    points, parts, count = back.shape[1:]
    first = back[0].reshape(points // 25, 5, 5, parts, count)
    second = back[1].reshape(points // 25, 5, 5, parts, count)
    term_s = jnp.einsum('aj,eabcm->ejbcm', deriv, first, precision=lax.Precision.HIGHEST).reshape(points, parts, count)
    term_z = jnp.einsum('bj,eabcm->eajcm', deriv, second, precision=lax.Precision.HIGHEST).reshape(points, parts, count)
    scale = orders.astype(jnp.float32)[None, :] / radius[:, None]
    third = back[2]
    beside_all = jnp.stack([-scale * third[:, 1], scale * third[:, 0]], axis=1)
    return term_s + term_z + beside_all

def reference(disp_now, disp_prev, kappa, radius, fwd_strain, order_bucket, shared_nodes, region_map):
    nphi = 2 * MAXO
    part_pts = 25 * E_DEV
    deriv_np, gllw_np = gll_tables()
    deriv = jnp.asarray(deriv_np, jnp.float32)
    orders = jnp.arange(MAXO, dtype=jnp.int32)
    samples = jnp.arange(nphi, dtype=jnp.int32)
    flat_table = fourier_table(orders, samples, nphi).reshape(2 * MAXO, nphi)
    mask = order_mask(order_bucket, orders)
    weight_pt = jnp.tile(jnp.asarray(gllw_np, jnp.float32), ELEMS) * radius
    quad = weight_pt * (2.0 * math.pi / nphi)
    zero_mode = jnp.zeros((2, MAXO), jnp.float32).at[0, 0].set(1.0)
    mass = weight_pt[:, None, None] * math.pi * (1.0 + zero_mode)[None]
    offsets = (jnp.arange(N_MER, dtype=jnp.int32) * part_pts)[:, None]
    left_glob = (shared_nodes[:, 0, :] + offsets)[1:].reshape(-1)
    right_glob = (shared_nodes[:, 1, :] + offsets)[:-1].reshape(-1)

    def partition_force(inputs):
        field, modulus, radius_part, quad_part, forward = inputs
        strain = strains(field, radius_part, orders, deriv).astype(jnp.bfloat16)
        phys = jnp.dot(strain.reshape(3 * part_pts, 2 * MAXO), flat_table, preferred_element_type=jnp.float32).reshape(3, part_pts, nphi)
        stress = (phys * modulus.astype(jnp.float32)[None] * quad_part[None, :, None]).astype(jnp.bfloat16)
        dens = lax.optimization_barrier(jnp.sum(phys * forward.astype(jnp.float32), axis=0)) * quad_part[:, None] * kernel_scale
        back = jnp.dot(stress.reshape(3 * part_pts, nphi), flat_table.T, preferred_element_type=jnp.float32).reshape(3, part_pts, 2, MAXO)
        return (divergence(back, radius_part, orders, deriv), dens)
    current = disp_now * mask
    previous = disp_prev * mask
    density = jnp.zeros((POINTS, nphi), jnp.float32)
    for section in range(STEPS):
        forward = fwd_strain[section].reshape(3, N_MER, part_pts, nphi).transpose(1, 0, 2, 3)
        force, dens = lax.map(partition_force, (current.reshape(N_MER, part_pts, 2, MAXO), kappa.reshape(N_MER, part_pts, nphi), radius.reshape(N_MER, part_pts), quad.reshape(N_MER, part_pts), forward))
        force = force.reshape(POINTS, 2, MAXO)
        density = density + dens.reshape(POINTS, nphi)
        assembled = force.at[right_glob].add(force[left_glob]).at[left_glob].add(force[right_glob])
        accel = -mask * assembled / mass
        current, previous = (2.0 * current - previous + time_step_sq * accel, current)
    sectors = density.reshape(POINTS, NSECT, nphi // NSECT).sum(axis=-1)
    region_pt = jnp.repeat(region_map, 25)
    kernel = jax.ops.segment_sum(sectors, region_pt, num_segments=NREG)
    return (current, kernel)
```

```python
import functools
import math

import jax
import jax.numpy as jnp
import numpy as np
from jax import lax
from jax.experimental import pallas as pl
from jax.experimental.pallas import tpu as pltpu
from jax.sharding import PartitionSpec as P

MAXO = 2048
STEPS = 2
PTS = 128
ELEM_ROWS = 8
TABLE_STRIDE = 64

time_step_sq = 0.0004
kernel_scale = 0.0001
bucket_orders = (8, 64, 512, 2048)

f32 = jnp.float32
bf16 = jnp.bfloat16


def gll_tables():
    nodes = np.array([-1.0, -math.sqrt(3.0 / 7.0), 0.0, math.sqrt(3.0 / 7.0), 1.0])
    weights_line = np.array([0.1, 49.0 / 90.0, 32.0 / 45.0, 49.0 / 90.0, 0.1])
    legendre = (35.0 * nodes**4 - 30.0 * nodes**2 + 3.0) / 8.0
    deriv = np.zeros((5, 5))
    for row_index in range(5):
        for col_index in range(5):
            if row_index != col_index:
                deriv[row_index, col_index] = (
                    legendre[row_index]
                    / legendre[col_index]
                    / (nodes[row_index] - nodes[col_index])
                )
    deriv[0, 0] = -5.0
    deriv[4, 4] = 5.0
    return (deriv, np.outer(weights_line, weights_line).reshape(25))


def split_const(x):
    high = np.asarray(x, np.float32).astype(bf16)
    low = (np.asarray(x, np.float32) - high.astype(np.float32)).astype(bf16)
    return high, low


def derivative_matrices(elements):
    deriv, _ = gll_tables()
    along_s = np.zeros((PTS, PTS))
    along_z = np.zeros((PTS, PTS))
    for e in range(elements):
        base = slice(25 * e, 25 * e + 25)
        along_s[base, base] = np.kron(deriv, np.eye(5))
        along_z[base, base] = np.kron(np.eye(5), deriv)
    both = np.concatenate([along_s, along_z])
    high, low = split_const(both)
    forward = np.concatenate([high, high, low], axis=1)
    high_t, low_t = split_const(both.T)
    return forward, np.concatenate([high_t, low_t], axis=1)


def small_tables(samples, nphi):
    coarse = TABLE_STRIDE * jnp.arange(MAXO // TABLE_STRIDE, dtype=jnp.int32)
    fine = jnp.arange(TABLE_STRIDE, dtype=jnp.int32)
    every = jnp.concatenate([coarse, fine])
    angle = (every[:, None] * samples[None, :] % nphi).astype(f32) * (2.0 * math.pi / nphi)
    both = jnp.stack([jnp.cos(angle), jnp.sin(angle)])
    return both[:, : coarse.shape[0]], both[:, coarse.shape[0] :]


def table_kernel(coarse_ref, fine_ref, out_ref):
    per_step = out_ref.shape[1] // TABLE_STRIDE
    fine_cos, fine_sin = fine_ref[0], fine_ref[1]
    for i in range(per_step):
        a = pl.program_id(0) * per_step + i
        big_cos = coarse_ref[0, pl.ds(a, 1), :]
        big_sin = coarse_ref[1, pl.ds(a, 1), :]
        rows = slice(i * TABLE_STRIDE, (i + 1) * TABLE_STRIDE)
        out_ref[0, rows, :] = (big_cos * fine_cos - big_sin * fine_sin).astype(bf16)
        out_ref[1, rows, :] = (big_sin * fine_cos + big_cos * fine_sin).astype(bf16)


def fourier_table(coarse, fine):
    count = coarse.shape[2]
    block = 4 * TABLE_STRIDE
    return pl.pallas_call(
        table_kernel,
        grid=(MAXO // block,),
        in_specs=[
            pl.BlockSpec(coarse.shape, lambda i: (0, 0, 0)),
            pl.BlockSpec(fine.shape, lambda i: (0, 0, 0)),
        ],
        out_specs=pl.BlockSpec((2, block, count), lambda i: (0, i, 0)),
        out_shape=jax.ShapeDtypeStruct((2, MAXO, count), bf16),
        name="table",
        cost_estimate=pl.CostEstimate(
            flops=6 * MAXO * count, bytes_accessed=4 * MAXO * count, transcendentals=0
        ),
    )(coarse, fine)


def dot(a, b):
    return jnp.dot(a, b, preferred_element_type=f32)


def dot_t(a, b):
    return lax.dot_general(a, b, (((1,), (1,)), ((), ())), preferred_element_type=f32)


def exact_dot(a, b):
    return jnp.dot(a, b, preferred_element_type=f32, precision=lax.Precision.HIGHEST)


def step_kernel(
    place_ref,
    u0_ref,
    u1_ref,
    u2_ref,
    u3_ref,
    kappa_ref,
    fwd_ref,
    table_ref,
    forward_ref,
    backward_ref,
    column_ref,
    sum_rows_ref,
    sum_cols_ref,
    before_ref,
    o0_ref,
    o1_ref,
    o2_ref,
    o3_ref,
    density_ref,
    coeff_ref,
    stress_ref,
):
    count = u0_ref.shape[2]
    samples = kappa_ref.shape[1]
    lane = lax.broadcasted_iota(jnp.int32, (1, count), 1)
    inv_radius = column_ref[:, 0:1]
    quad = column_ref[:, 1:2]
    for shift, u_ref in enumerate((u0_ref, u1_ref, u2_ref, u3_ref)):
        start = pl.multiple_of(place_ref[0, shift], count)
        order = (lane + start).astype(f32)
        u0, u1 = u_ref[0], u_ref[1]
        coeff_ref[:PTS, pl.ds(start, count)] = u0
        coeff_ref[:PTS, pl.ds(MAXO + start, count)] = u1
        coeff_ref[PTS:, pl.ds(start, count)] = (order * u1.astype(f32)).astype(bf16)
        coeff_ref[PTS:, pl.ds(MAXO + start, count)] = (-order * u0.astype(f32)).astype(bf16)
    forward, backward = forward_ref[...], backward_ref[...]
    width = 256
    density = before_ref[...]
    for n in range(samples // width):
        cols = slice(n * width, (n + 1) * width)
        phys = dot(coeff_ref[:, :MAXO], table_ref[0, :, cols]) + dot(
            coeff_ref[:, MAXO:], table_ref[1, :, cols]
        )
        field, around = phys[:PTS], phys[PTS:] * inv_radius
        high = field.astype(bf16)
        low = (field - high.astype(f32)).astype(bf16)
        along = dot(forward, jnp.concatenate([high, low, high]))
        along_s, along_z = along[:PTS], along[PTS:]
        modulus = kappa_ref[:, cols].astype(f32) * quad
        stress = jnp.concatenate([along_s * modulus, along_z * modulus]).astype(bf16)
        stress_ref[:PTS, cols] = dot(backward, jnp.concatenate([stress, stress])).astype(bf16)
        stress_ref[PTS:, cols] = (around * modulus * inv_radius).astype(bf16)
        dens = (
            along_s * fwd_ref[0, :, cols].astype(f32)
            + along_z * fwd_ref[1, :, cols].astype(f32)
            + around * fwd_ref[2, :, cols].astype(f32)
        ) * (quad * kernel_scale)
        by_element = exact_dot(sum_rows_ref[...], dens)
        density = density + exact_dot(by_element, sum_cols_ref[cols, :])
    density_ref[...] = density
    for shift, o_ref in enumerate((o0_ref, o1_ref, o2_ref, o3_ref)):
        start = pl.multiple_of(place_ref[1, shift], count)
        order = (lane + start).astype(f32)
        cosine = dot_t(stress_ref[...], table_ref[0, pl.ds(start, count), :])
        sine = dot_t(stress_ref[...], table_ref[1, pl.ds(start, count), :])
        o_ref[0] = (cosine[:PTS] - order * sine[PTS:]).astype(bf16)
        o_ref[1] = (sine[:PTS] + order * cosine[PTS:]).astype(bf16)


def step_call(place, blocks, kappa, fwd, table, consts, columns, before):
    count = blocks[0].shape[2]
    samples = kappa.shape[1]
    vmem = pl.BlockSpec(memory_space=pltpu.VMEM)
    smem = pl.BlockSpec(memory_space=pltpu.SMEM)
    out_block = jax.ShapeDtypeStruct((2, PTS, count), bf16)
    flops = 2 * 2 * 2 * PTS * 2 * MAXO * samples
    return pl.pallas_call(
        step_kernel,
        in_specs=[smem] + [vmem] * 13,
        out_specs=[vmem] * 5,
        out_shape=[out_block] * 4 + [jax.ShapeDtypeStruct(before.shape, f32)],
        scratch_shapes=[
            pltpu.VMEM((2 * PTS, 2 * MAXO), bf16),
            pltpu.VMEM((2 * PTS, samples), bf16),
        ],
        name="step",
        compiler_params=pltpu.CompilerParams(vmem_limit_bytes=40 * 1024 * 1024),
        cost_estimate=pl.CostEstimate(
            flops=flops, bytes_accessed=4 * MAXO * samples, transcendentals=0
        ),
    )(place, *blocks, kappa, fwd, table, consts[0], consts[1], columns, consts[2], consts[3], before)


def gather_rows_kernel(nodes_ref, a_ref, b_ref, c_ref, d_ref, force_ref, left_ref, right_ref):
    force_ref[...] = (
        a_ref[...].astype(f32) + b_ref[...].astype(f32) + c_ref[...].astype(f32) + d_ref[...].astype(f32)
    )
    for side, o_ref in enumerate((left_ref, right_ref)):
        for k in range(nodes_ref.shape[1]):
            row = nodes_ref[side, k]
            for c in range(2):
                o_ref[c, k : k + 1, :] = force_ref[c, pl.ds(row, 1), :]


def gather_rows(nodes, parts):
    vmem = pl.BlockSpec(memory_space=pltpu.VMEM)
    smem = pl.BlockSpec(memory_space=pltpu.SMEM)
    count = parts[0].shape[2]
    rows = jax.ShapeDtypeStruct((2, nodes.shape[1], count), f32)
    return pl.pallas_call(
        gather_rows_kernel,
        in_specs=[smem] + [vmem] * 4,
        out_specs=[vmem] * 3,
        out_shape=[jax.ShapeDtypeStruct((2, PTS, count), f32), rows, rows],
        name="rows",
    )(nodes, *parts)


def update_kernel(
    nodes_ref, place_ref, force_ref, before_ref, after_ref, now_ref, prev_ref, column_ref, next_ref, send_ref, total_ref
):
    total_ref[...] = force_ref[...]
    for side, r_ref in enumerate((before_ref, after_ref)):
        for k in range(nodes_ref.shape[1]):
            row = nodes_ref[side, k]
            for c in range(2):
                total_ref[c, pl.ds(row, 1), :] += r_ref[c, k : k + 1, :]
    shape = total_ref.shape[1:]
    order = lax.broadcasted_iota(jnp.int32, shape, 1) + place_ref[0, 0]
    level = column_ref[:, 2:3]
    scale = column_ref[:, 3:4]
    inside = order.astype(f32) < level
    first = order == 0
    for c in range(2):
        gain = jnp.where(first, scale * (0.5 if c == 0 else 0.0), scale)
        gain = jnp.where(inside, gain, 0.0)
        value = 2.0 * now_ref[c] - prev_ref[c] - gain * total_ref[c]
        next_ref[c] = value
        send_ref[c] = value.astype(bf16)


def update(nodes, place, force, before, after, now, prev, columns):
    vmem = pl.BlockSpec(memory_space=pltpu.VMEM)
    smem = pl.BlockSpec(memory_space=pltpu.SMEM)
    return pl.pallas_call(
        update_kernel,
        in_specs=[smem, smem] + [vmem] * 6,
        out_specs=[vmem] * 2,
        out_shape=[jax.ShapeDtypeStruct(force.shape, f32), jax.ShapeDtypeStruct(force.shape, bf16)],
        scratch_shapes=[pltpu.VMEM(force.shape, f32)],
        name="update",
    )(nodes, place, force, before, after, now, prev, columns)


def owners_kernel(first_ref, rows_ref, out_ref):
    regions, sectors = out_ref.shape
    ids = rows_ref[:, sectors : sectors + 1]
    mine = lax.broadcasted_iota(jnp.int32, (rows_ref.shape[0], regions), 1) + first_ref[0, 0]
    chosen = jnp.where(ids == mine.astype(f32), 1.0, 0.0)
    out_ref[...] = lax.dot_general(
        chosen,
        rows_ref[:, :sectors],
        (((0,), (0,)), ((), ())),
        preferred_element_type=f32,
        precision=lax.Precision.HIGHEST,
    )


def owners(first, rows, regions, sectors):
    return pl.pallas_call(
        owners_kernel,
        in_specs=[pl.BlockSpec(memory_space=pltpu.SMEM), pl.BlockSpec(memory_space=pltpu.VMEM)],
        out_specs=pl.BlockSpec(memory_space=pltpu.VMEM),
        out_shape=jax.ShapeDtypeStruct((regions, sectors), f32),
        name="owners",
    )(first, rows)


def turned(x, by):
    devices = lax.axis_size("blk")
    return lax.ppermute(x, "blk", [(i, (i + by) % devices) for i in range(devices)])


def shifted(x, by):
    devices = lax.axis_size("mer")
    pairs = [(i, i + by) for i in range(devices) if 0 <= i + by < devices]
    return lax.ppermute(x, "mer", pairs)


def everyone(x):
    devices = lax.axis_size("mer")
    x_bits = [8, 16, 32, 2, 4, 1]
    assert devices == 64
    for bit in x_bits:
        other = lax.ppermute(x, "mer", [(i, i ^ bit) for i in range(devices)])
        x = jnp.concatenate([x, other])
    return x


def local(disp_now, disp_prev, kappa, radius, fwd_strain, order_bucket, shared_nodes, region_map):
    points, _, count = disp_now.shape
    elements = order_bucket.shape[0]
    samp_count = kappa.shape[1]
    nphi = 2 * MAXO
    sectors = samp_count // 4
    regions = 4096 // lax.axis_size("mer")
    blk = lax.axis_index("blk")
    mer = lax.axis_index("mer")
    pad = PTS - points

    levels = jnp.zeros(order_bucket.shape, jnp.int32)
    for position, value in enumerate(bucket_orders):
        levels = levels + jnp.where(order_bucket == position, value, 0).astype(jnp.int32)
    levels = jnp.repeat(levels, 25)
    orders = blk * count + jnp.arange(count, dtype=jnp.int32)
    cosine_part = orders[None, :] < levels[:, None]
    mask = jnp.stack([cosine_part, cosine_part & (orders[None, :] >= 1)])

    def arranged(disp):
        return jnp.pad(jnp.where(mask, disp.transpose(1, 0, 2), 0.0), ((0, 0), (0, pad), (0, 0)))

    current = arranged(disp_now)
    previous = arranged(disp_prev)
    send = current.astype(bf16)

    _, gllw = gll_tables()
    weight = jnp.tile(jnp.asarray(gllw, f32), elements) * radius
    columns = jnp.stack(
        [
            1.0 / radius,
            weight * (2.0 * math.pi / nphi),
            levels.astype(f32),
            time_step_sq / (weight * math.pi),
        ],
        axis=1,
    )
    columns = jnp.pad(columns, ((0, pad), (0, 0)))
    table = fourier_table(*small_tables(blk * samp_count + jnp.arange(samp_count, dtype=jnp.int32), nphi))
    kappa = jnp.pad(kappa, ((0, pad), (0, 0)))
    fwd = jnp.pad(fwd_strain, ((0, 0), (0, 0), (0, pad), (0, 0)))
    forward, backward = derivative_matrices(elements)
    sum_rows = np.zeros((ELEM_ROWS, PTS), np.float32)
    for e in range(elements):
        sum_rows[e, 25 * e : 25 * e + 25] = 1.0
    sum_cols = np.kron(np.eye(sectors), np.ones((4, 1))).astype(np.float32)
    consts = tuple(jnp.asarray(x) for x in (forward, backward, sum_rows, sum_cols))
    shifts = (0, 1, 3, 2)
    nblk = lax.axis_size("blk")
    place = jnp.stack(
        [
            jnp.stack([(blk - s) % nblk * count for s in shifts]),
            jnp.stack([(blk + s) % nblk * count for s in shifts]),
        ]
    ).astype(jnp.int32)
    nodes = shared_nodes[0]
    density = jnp.zeros((ELEM_ROWS, sectors), f32)
    for section in range(STEPS):
        blocks = [send] + [turned(send, s) for s in shifts[1:]]
        *forces, density = step_call(place, blocks, kappa, fwd[section], table, consts, columns, density)
        parts = [forces[0]] + [turned(x, s) for x, s in zip(forces[1:], shifts[1:])]
        force, left, right = gather_rows(nodes, parts)
        from_next = shifted(left, -1)
        from_before = shifted(right, 1)
        following, send = update(nodes, place, force, from_before, from_next, current, previous, columns)
        current, previous = following, current
    ids = jnp.pad(region_map.astype(f32), (0, ELEM_ROWS - elements), constant_values=-1.0)
    rows = jnp.concatenate([density, jnp.broadcast_to(ids[:, None], (ELEM_ROWS, 128))], axis=1)
    first = (mer * regions).astype(jnp.int32).reshape(1, 1)
    kernel = owners(first, everyone(rows), regions, sectors)
    displacement = current[:, :points].transpose(1, 0, 2)
    return (displacement, kernel)


def solution(mesh):
    in_specs = (
        P("mer", None, "blk"),
        P("mer", None, "blk"),
        P("mer", "blk"),
        P("mer"),
        P(None, None, "mer", "blk"),
        P("mer"),
        P("mer", None, None),
        P("mer"),
    )
    out_specs = (P("mer", None, "blk"), P("mer", "blk"))
    return jax.shard_map(local, mesh=mesh, in_specs=in_specs, out_specs=out_specs, check_vma=False)
```

```python
import functools
import math

import jax
import jax.numpy as jnp
import numpy as np
from jax import lax
from jax.experimental import pallas as pl
from jax.experimental.pallas import tpu as pltpu
from jax.sharding import PartitionSpec as P

MAXO = 2048
STEPS = 2
PTS = 128
ELEM_ROWS = 8
ID_ROW = 5
TABLE_STRIDE = 64
PARTNERS = (0, 2, 1, 3)

time_step_sq = 0.0004
kernel_scale = 0.0001
bucket_orders = (8, 64, 512, 2048)

f32 = jnp.float32
bf16 = jnp.bfloat16


def gll_tables():
    nodes = np.array([-1.0, -math.sqrt(3.0 / 7.0), 0.0, math.sqrt(3.0 / 7.0), 1.0])
    weights_line = np.array([0.1, 49.0 / 90.0, 32.0 / 45.0, 49.0 / 90.0, 0.1])
    legendre = (35.0 * nodes**4 - 30.0 * nodes**2 + 3.0) / 8.0
    deriv = np.zeros((5, 5))
    for row_index in range(5):
        for col_index in range(5):
            if row_index != col_index:
                deriv[row_index, col_index] = (
                    legendre[row_index]
                    / legendre[col_index]
                    / (nodes[row_index] - nodes[col_index])
                )
    deriv[0, 0] = -5.0
    deriv[4, 4] = 5.0
    return (deriv, np.outer(weights_line, weights_line).reshape(25))


def split_const(x):
    high = np.asarray(x, np.float32).astype(bf16)
    low = (np.asarray(x, np.float32) - high.astype(np.float32)).astype(bf16)
    return high, low


def derivative_matrices(elements):
    deriv, _ = gll_tables()
    along_s = np.zeros((PTS, PTS))
    along_z = np.zeros((PTS, PTS))
    for e in range(elements):
        base = slice(25 * e, 25 * e + 25)
        along_s[base, base] = np.kron(deriv, np.eye(5))
        along_z[base, base] = np.kron(np.eye(5), deriv)
    both = np.concatenate([along_s, along_z])
    high, low = split_const(both)
    forward = np.concatenate([high, high, low], axis=1)
    high_t, low_t = split_const(both.T)
    return forward, np.concatenate([high_t, low_t], axis=1)


def small_tables(nphi):
    coarse = TABLE_STRIDE * np.arange(MAXO // TABLE_STRIDE)
    every = np.concatenate([coarse, np.arange(TABLE_STRIDE)])
    angle = (every[:, None] * np.arange(nphi)[None, :] % nphi) * (2.0 * math.pi / nphi)
    return np.stack([np.cos(angle), np.sin(angle)]).astype(np.float32)


def table_kernel(small_ref, out_ref):
    coarse = MAXO // TABLE_STRIDE

    def one(a, carry):
        big_cos = small_ref[0, pl.ds(a, 1), :]
        big_sin = small_ref[1, pl.ds(a, 1), :]
        start = pl.multiple_of(a * TABLE_STRIDE, TABLE_STRIDE)
        for part in range(0, TABLE_STRIDE, 16):
            fine_cos = small_ref[0, coarse + part : coarse + part + 16, :]
            fine_sin = small_ref[1, coarse + part : coarse + part + 16, :]
            rows = pl.ds(pl.multiple_of(start + part, 16), 16)
            out_ref[0, rows, :] = (big_cos * fine_cos - big_sin * fine_sin).astype(bf16)
            out_ref[1, rows, :] = (big_sin * fine_cos + big_cos * fine_sin).astype(bf16)
        return carry

    lax.fori_loop(0, coarse, one, 0)


VMEM = pl.BlockSpec(memory_space=pltpu.VMEM)
SMEM = pl.BlockSpec(memory_space=pltpu.SMEM)


def call(kernel, name, out_shape, operands, scalars=0, scratch=(), mib=16):
    single = not isinstance(out_shape, (list, tuple))
    return pl.pallas_call(
        kernel,
        in_specs=[SMEM] * scalars + [VMEM] * (len(operands) - scalars),
        out_specs=VMEM if single else [VMEM] * len(out_shape),
        out_shape=out_shape,
        scratch_shapes=list(scratch),
        name=name,
        compiler_params=pltpu.CompilerParams(vmem_limit_bytes=mib * 1024 * 1024),
    )(*operands)


def block_start(blk_ref, bits, count):
    blk = blk_ref[0, 0]
    partner = (blk, blk + 1 - 2 * lax.rem(blk, 2), lax.rem(blk + 2, 4), 3 - blk)[bits]
    return pl.multiple_of(partner * count, count)


def fourier_table(small):
    count = small.shape[2]
    shape = jax.ShapeDtypeStruct((2, MAXO, count), bf16)
    return call(table_kernel, "table", shape, [small])


def dot(a, b):
    return jnp.dot(a, b, preferred_element_type=f32)


def dot_t(a, b):
    return lax.dot_general(a, b, (((1,), (1,)), ((), ())), preferred_element_type=f32)


def exact_dot(a, b):
    return jnp.dot(a, b, preferred_element_type=f32, precision=lax.Precision.HIGHEST)


def levels_of(bucket_ref, points):
    point = lax.broadcasted_iota(jnp.int32, (points, 1), 0)
    level = jnp.zeros((points, 1), jnp.int32)
    for e in range(bucket_ref.shape[1]):
        value = jnp.int32(0)
        for position, orders in enumerate(bucket_orders):
            value = jnp.where(bucket_ref[0, e] == position, orders, value)
        level = jnp.where((point >= 25 * e) & (point < 25 * e + 25), value, level)
    return level


def arrange_kernel(bucket_ref, blk_ref, disp_ref, now_ref, *send_ref):
    points, _, count = disp_ref.shape
    order = lax.broadcasted_iota(jnp.int32, (points, count), 1) + blk_ref[0, 0] * count
    inside = order < levels_of(bucket_ref, points)
    now_ref[:, points:, :] = jnp.zeros((2, now_ref.shape[1] - points, count), f32)
    for c in range(2):
        kept = inside if c == 0 else inside & (order >= 1)
        now_ref[c, :points, :] = jnp.where(kept, disp_ref[:, c, :], 0.0)
    for s_ref in send_ref:
        s_ref[...] = now_ref[...].astype(bf16)


def arrange(buckets, blk, disp, with_send):
    shape = (2, PTS, disp.shape[2])
    outs = [jax.ShapeDtypeStruct(shape, f32)] + [jax.ShapeDtypeStruct(shape, bf16)] * with_send
    return call(arrange_kernel, "arrange", outs, [buckets, blk, disp], 2)


def setup_kernel(bucket_ref, region_ref, radius_ref, weight_ref, kappa_ref, fwd_ref, column_ref, kap_ref, first_ref, second_ref, density_ref):
    points = radius_ref.shape[1]
    square = (points, points)
    diagonal = lax.broadcasted_iota(jnp.int32, square, 0) == lax.broadcasted_iota(jnp.int32, square, 1)
    radius = jnp.sum(jnp.where(diagonal, radius_ref[...], 0.0), axis=1, keepdims=True)
    weight = weight_ref[...] * radius
    column_ref[...] = jnp.zeros(column_ref.shape, f32)
    column_ref[:points, 0:1] = 1.0 / radius
    column_ref[:points, 1:2] = weight * (2.0 * math.pi / (2 * MAXO))
    column_ref[:points, 2:3] = levels_of(bucket_ref, points).astype(f32)
    column_ref[:points, 3:4] = time_step_sq / (weight * math.pi)
    tail = PTS - 16
    kap_ref[tail:, :] = jnp.zeros((16, kap_ref.shape[1]), bf16)
    kap_ref[:points, :] = kappa_ref[...]
    for s, o_ref in enumerate((first_ref, second_ref)):
        for i in range(3):
            o_ref[i, tail:, :] = jnp.zeros((16, kap_ref.shape[1]), bf16)
            o_ref[i, :points, :] = fwd_ref[s, i]
    shape = density_ref.shape
    row, lane = lax.broadcasted_iota(jnp.int32, shape, 0), lax.broadcasted_iota(jnp.int32, shape, 1)
    density = jnp.zeros(shape, f32)
    for e in range(region_ref.shape[1]):
        name = region_ref[0, e].astype(f32)
        density = jnp.where((row == ID_ROW) & (lane == e), name, density)
    density_ref[...] = density


def setup(buckets, regions, radius, weight, kappa, fwd):
    samples = kappa.shape[1]
    outs = [
        jax.ShapeDtypeStruct((PTS, 4), f32),
        jax.ShapeDtypeStruct((PTS, samples), bf16),
        jax.ShapeDtypeStruct((3, PTS, samples), bf16),
        jax.ShapeDtypeStruct((3, PTS, samples), bf16),
        jax.ShapeDtypeStruct((ELEM_ROWS, samples // 4), f32),
    ]
    return call(setup_kernel, "setup", outs, [buckets, regions, radius, weight, kappa, fwd], 2)


def sides(mer_ref):
    here = 1 - lax.rem(mer_ref[0, 0], 2)
    return here, 1 - here


def synthesis_kernel(
    blk_ref,
    mer_ref,
    nodes_ref,
    u0_ref,
    u1_ref,
    u2_ref,
    u3_ref,
    kappa_ref,
    fwd_ref,
    table_ref,
    forward_ref,
    backward_ref,
    column_ref,
    sum_rows_ref,
    sum_cols_ref,
    before_ref,
    stress_ref,
    core_ref,
    chip_ref,
    density_ref,
    coeff_ref,
    dens_ref,
):
    count = u0_ref.shape[2]
    samples = kappa_ref.shape[1]
    lane = lax.broadcasted_iota(jnp.int32, (1, count), 1)
    inv_radius = column_ref[:, 0:1]
    quad = column_ref[:, 1:2]
    for bits, u_ref in zip(PARTNERS, (u0_ref, u1_ref, u2_ref, u3_ref)):
        start = block_start(blk_ref, bits, count)
        order = (lane + start).astype(f32)
        u0, u1 = u_ref[0], u_ref[1]
        coeff_ref[:PTS, pl.ds(start, count)] = u0
        coeff_ref[:PTS, pl.ds(MAXO + start, count)] = u1
        coeff_ref[PTS:, pl.ds(start, count)] = (order * u1.astype(f32)).astype(bf16)
        coeff_ref[PTS:, pl.ds(MAXO + start, count)] = (-order * u0.astype(f32)).astype(bf16)
    width = 1024
    for n in range(samples // width):
        cols = slice(n * width, (n + 1) * width)
        phys = dot(coeff_ref[:, :MAXO], table_ref[0, :, cols]) + dot(
            coeff_ref[:, MAXO:], table_ref[1, :, cols]
        )
        field, around = phys[:PTS], phys[PTS:] * inv_radius
        high = field.astype(bf16)
        low = (field - high.astype(f32)).astype(bf16)
        along = dot(forward_ref[...], jnp.concatenate([high, low, high]))
        along_s, along_z = along[:PTS], along[PTS:]
        modulus = kappa_ref[:, cols].astype(f32) * quad
        stress = jnp.concatenate([along_s * modulus, along_z * modulus]).astype(bf16)
        stress_ref[:PTS, cols] = dot(backward_ref[...], jnp.concatenate([stress, stress]))
        stress_ref[PTS:, cols] = around * modulus * inv_radius
        dens = (
            along_s * fwd_ref[0, :, cols].astype(f32)
            + along_z * fwd_ref[1, :, cols].astype(f32)
            + around * fwd_ref[2, :, cols].astype(f32)
        ) * (quad * kernel_scale)
        dens_high = dens.astype(bf16)
        dens_ref[:PTS, cols] = dens_high
        dens_ref[PTS:, cols] = (dens - dens_high.astype(f32)).astype(bf16)
    spare = jnp.zeros((8 - nodes_ref.shape[1], samples), f32)
    for o_ref, side in zip((core_ref, chip_ref), sides(mer_ref)):
        rows = []
        for part in range(2):
            for k in range(nodes_ref.shape[1]):
                rows.append(stress_ref[pl.ds(PTS * part + nodes_ref[side, k], 1), :])
            rows.append(spare)
        o_ref[...] = jnp.concatenate(rows).astype(bf16)
    by_sector = dot(dens_ref[...], sum_cols_ref[...])
    density_ref[...] = before_ref[...] + exact_dot(sum_rows_ref[...], by_sector[:PTS] + by_sector[PTS:])


def synthesis(blk, mer, nodes, blocks, kappa, fwd, table, consts, columns, before):
    forward, backward, sum_rows, sum_cols = consts
    samples = kappa.shape[1]
    rows = jax.ShapeDtypeStruct((16, samples), bf16)
    outs = [jax.ShapeDtypeStruct((2 * PTS, samples), f32), rows, rows, jax.ShapeDtypeStruct(before.shape, f32)]
    scratch = [pltpu.VMEM((2 * PTS, 2 * MAXO), bf16), pltpu.VMEM((2 * PTS, samples), bf16)]
    operands = [blk, mer, nodes, *blocks, kappa, fwd, table, forward, backward, columns, sum_rows, sum_cols, before]
    return call(synthesis_kernel, "synthesis", outs, operands, 3, scratch)


def merge_kernel(mer_ref, nodes_ref, stress_ref, core_ref, chip_ref, out_ref, total_ref):
    total_ref[...] = stress_ref[...]
    for r_ref, side in zip((core_ref, chip_ref), sides(mer_ref)):
        rows = r_ref[...].astype(f32)
        for part in range(2):
            for k in range(nodes_ref.shape[1]):
                at = 8 * part + k
                total_ref[pl.ds(PTS * part + nodes_ref[side, k], 1), :] += rows[at : at + 1]
    out_ref[...] = total_ref[...].astype(bf16)


def merge(mer, nodes, stress, core, chip):
    shape = jax.ShapeDtypeStruct(stress.shape, bf16)
    scratch = [pltpu.VMEM(stress.shape, f32)]
    return call(merge_kernel, "merge", shape, [mer, nodes, stress, core, chip], 2, scratch)


def analysis_kernel(shift, blk_ref, stress_ref, table_ref, o_ref):
    count = o_ref.shape[2]
    start = block_start(blk_ref, shift, count)
    order = (lax.broadcasted_iota(jnp.int32, (1, count), 1) + start).astype(f32)
    cosine = dot_t(stress_ref[...], table_ref[0, pl.ds(start, count), :])
    sine = dot_t(stress_ref[...], table_ref[1, pl.ds(start, count), :])
    o_ref[0] = (cosine[:PTS] - order * sine[PTS:]).astype(bf16)
    o_ref[1] = (sine[:PTS] + order * cosine[PTS:]).astype(bf16)


def analysis(shift, blk, stress, table, count):
    shape = jax.ShapeDtypeStruct((2, PTS, count), bf16)
    kernel = functools.partial(analysis_kernel, shift)
    return call(kernel, "analysis", shape, [blk, stress, table], 1)


def update_kernel(blk_ref, *refs):
    parts = refs[:4]
    now_ref, prev_ref, column_ref = refs[4:7]
    outs = refs[7:]
    shape = now_ref.shape[1:]
    order = lax.broadcasted_iota(jnp.int32, shape, 1) + blk_ref[0, 0] * shape[1]
    level = column_ref[:, 2:3]
    scale = column_ref[:, 3:4]
    inside = order.astype(f32) < level
    first = order == 0
    for c in range(2):
        gain = jnp.where(first, scale * (0.5 if c == 0 else 0.0), scale)
        gain = jnp.where(inside, gain, 0.0)
        force = sum(p[c].astype(f32) for p in parts)
        value = 2.0 * now_ref[c] - prev_ref[c] - gain * force
        if len(outs) == 2:
            outs[0][c] = value
            outs[1][c] = value.astype(bf16)
        else:
            points = outs[0].shape[0]
            outs[0][:, c, :] = value[:points]


def update(blk, parts, now, prev, columns, points):
    if points:
        outs = [jax.ShapeDtypeStruct((points, 2, now.shape[2]), f32)]
    else:
        outs = [jax.ShapeDtypeStruct(now.shape, f32), jax.ShapeDtypeStruct(now.shape, bf16)]
    return call(update_kernel, "update", outs, [blk, *parts, now, prev, columns], 1)


def join_kernel(*refs):
    rows = refs[0].shape[0]
    for i, ref in enumerate(refs[:-1]):
        refs[-1][i * rows : (i + 1) * rows] = ref[...]


def joined(x, axis, *bits):
    pieces = [x] + [swapped(x, axis, b) for b in bits]
    shape = jax.ShapeDtypeStruct((len(pieces) * x.shape[0], x.shape[1]), x.dtype)
    return call(join_kernel, "join", shape, pieces)


def owners_kernel(first_ref, rows_ref, out_ref):
    regions, sectors = out_ref.shape
    count = rows_ref.shape[0]
    rows = rows_ref[...]
    names = rows[:, :128].reshape(count // ELEM_ROWS, ELEM_ROWS, 128)
    names = jnp.broadcast_to(names[:, ID_ROW : ID_ROW + 1], names.shape)
    element = lax.broadcasted_iota(jnp.int32, names.shape, 1)
    lane = lax.broadcasted_iota(jnp.int32, names.shape, 2)
    ids = jnp.sum(jnp.where((lane == element) & (element < ID_ROW), names, 0.0), axis=2, keepdims=True)
    ids = jnp.where(element[:, :, :1] < ID_ROW, ids, -1.0).reshape(count, 1)
    mine = (lax.broadcasted_iota(jnp.int32, (count, regions), 1) + first_ref[0, 0]).astype(f32)
    out_ref[...] = lax.dot_general(
        jnp.where(ids == mine, 1.0, 0.0),
        rows,
        (((0,), (0,)), ((), ())),
        preferred_element_type=f32,
        precision=lax.Precision.HIGHEST,
    )


def owners(first, rows, regions):
    shape = jax.ShapeDtypeStruct((regions, rows.shape[1]), f32)
    return call(owners_kernel, "owners", shape, [first, rows], 1)


def swapped(x, axis, bits):
    return lax.ppermute(x, axis, [(i, i ^ bits) for i in range(lax.axis_size(axis))])


def across_chips(x):
    ends = range(1, lax.axis_size("mer") - 1)
    return lax.ppermute(x, "mer", [(i, i + 1 if i % 2 else i - 1) for i in ends])


def tied(x, other):
    return lax.optimization_barrier((x, other))[0]


def local(disp_now, disp_prev, kappa, radius, fwd_strain, order_bucket, shared_nodes, region_map):
    points, _, count = disp_now.shape
    elements = order_bucket.shape[0]
    samp_count = kappa.shape[1]
    nphi = 2 * MAXO
    sectors = samp_count // 4
    regions = 4096 // lax.axis_size("mer")
    blk_index = lax.axis_index("blk").astype(jnp.int32)
    blk = blk_index.reshape(1, 1)
    mer = lax.axis_index("mer").astype(jnp.int32).reshape(1, 1)
    first = (lax.axis_index("mer").astype(jnp.int32) * regions).reshape(1, 1)
    buckets = order_bucket.reshape(1, -1)
    nodes = shared_nodes[0]
    current, send = arrange(buckets, blk, disp_now, 1)
    (previous,) = arrange(buckets, blk, disp_prev, 0)
    _, gllw = gll_tables()
    weight = jnp.asarray(np.tile(gllw, elements).reshape(-1, 1), f32)
    columns, kappa, *fwd, density = setup(
        buckets, region_map.reshape(1, -1), radius.reshape(1, -1), weight, kappa, fwd_strain
    )
    forward, backward = derivative_matrices(elements)
    sum_rows = np.zeros((ELEM_ROWS, PTS), np.float32)
    for e in range(elements):
        sum_rows[e, 25 * e : 25 * e + 25] = 1.0
    sum_cols = np.kron(np.eye(sectors), np.ones((4, 1))).astype(bf16)
    consts = tuple(jnp.asarray(x) for x in (forward, backward, sum_rows, sum_cols))
    small = lax.dynamic_slice_in_dim(jnp.asarray(small_tables(nphi)), blk_index * samp_count, samp_count, 2)
    small, columns, kappa, fwd, density, previous, first, consts = lax.optimization_barrier(
        (small, columns, kappa, fwd, density, previous, first, consts)
    )
    table = fourier_table(small)
    for section in range(STEPS):
        last = section == STEPS - 1
        blocks = [send] + [swapped(send, "blk", bits) for bits in PARTNERS[1:]]
        stress, core, chip, density = synthesis(
            blk, mer, nodes, blocks, kappa, fwd[section], table, consts, columns, density
        )
        if last:
            gathered = joined(density, "mer", 8, 16, 24)
            stress = tied(stress, gathered)
        chip, core = across_chips(chip), swapped(core, "mer", 1)
        stress = merge(mer, nodes, stress, core, chip)
        forces = {bits: analysis(bits, blk, stress, table, count) for bits in (2, 1)}
        if last:
            gathered = joined(tied(gathered, stress), "mer", 32)
            stress = tied(stress, gathered)
        forces |= {bits: analysis(bits, blk, stress, table, count) for bits in (3, 0)}
        parts = [forces[0]] + [swapped(forces[bits], "blk", bits) for bits in PARTNERS[1:]]
        if last:
            gathered = joined(tied(gathered, [parts[1], forces[1], forces[3], forces[0]]), "mer", 2, 4, 6)
            gathered = joined(gathered, "mer", 1)
        outs = update(blk, parts, current, previous, columns, points if last else 0)
        if not last:
            current, previous, send = outs[0], current, outs[1]
    return (outs[0], owners(first, gathered, regions))


def solution(mesh):
    in_specs = (
        P("mer", None, "blk"),
        P("mer", None, "blk"),
        P("mer", "blk"),
        P("mer"),
        P(None, None, "mer", "blk"),
        P("mer"),
        P("mer", None, None),
        P("mer"),
    )
    out_specs = (P("mer", None, "blk"), P("mer", "blk"))
    return jax.shard_map(local, mesh=mesh, in_specs=in_specs, out_specs=out_specs, check_vma=False)
```

```python
import functools
import math

import jax
import jax.numpy as jnp
import numpy as np
from jax import lax
from jax.experimental import pallas as pl
from jax.experimental.pallas import tpu as pltpu
from jax.sharding import PartitionSpec as P

MAXO = 2048
STEPS = 2
PIECES = 2
PTS = 128
ELEM_ROWS = 8
ID_ROW = 5
TABLE_STRIDE = 64
FLOPS_US = 1150000000
PARTNERS = (0, 2, 1, 3)

time_step_sq = 0.0004
kernel_scale = 0.0001
bucket_orders = (8, 64, 512, 2048)

f32 = jnp.float32
bf16 = jnp.bfloat16


def gll_tables():
    nodes = np.array([-1.0, -math.sqrt(3.0 / 7.0), 0.0, math.sqrt(3.0 / 7.0), 1.0])
    weights_line = np.array([0.1, 49.0 / 90.0, 32.0 / 45.0, 49.0 / 90.0, 0.1])
    legendre = (35.0 * nodes**4 - 30.0 * nodes**2 + 3.0) / 8.0
    deriv = np.zeros((5, 5))
    for row_index in range(5):
        for col_index in range(5):
            if row_index != col_index:
                deriv[row_index, col_index] = (
                    legendre[row_index]
                    / legendre[col_index]
                    / (nodes[row_index] - nodes[col_index])
                )
    deriv[0, 0] = -5.0
    deriv[4, 4] = 5.0
    return (deriv, np.outer(weights_line, weights_line).reshape(25))


def split_const(x):
    high = np.asarray(x, np.float32).astype(bf16)
    low = (np.asarray(x, np.float32) - high.astype(np.float32)).astype(bf16)
    return high, low


def derivative_matrices(elements):
    deriv, _ = gll_tables()
    along_s = np.zeros((PTS, PTS))
    along_z = np.zeros((PTS, PTS))
    for e in range(elements):
        base = slice(25 * e, 25 * e + 25)
        along_s[base, base] = np.kron(deriv, np.eye(5))
        along_z[base, base] = np.kron(np.eye(5), deriv)
    both = np.concatenate([along_s, along_z])
    high, low = split_const(both)
    forward = np.concatenate([high, high, low], axis=1)
    high_t, low_t = split_const(both.T)
    return forward, np.concatenate([high_t, low_t], axis=1)


def small_tables(samples):
    coarse = TABLE_STRIDE * np.arange(MAXO // TABLE_STRIDE)
    every = np.concatenate([coarse, np.arange(TABLE_STRIDE)])
    angle = (every[:, None] * np.arange(samples)[None, :] % (2 * MAXO)) * (math.pi / MAXO)
    return np.stack([np.cos(angle), np.sin(angle)]).astype(np.float32)


def table_kernel(blk_ref, small_ref, out_ref, fine_ref):
    coarse = MAXO // TABLE_STRIDE
    quarters = lax.broadcasted_iota(jnp.int32, (TABLE_STRIDE, 1), 0) * blk_ref[0, 0]
    quarters = jnp.bitwise_and(quarters, 3)
    by_cos = jnp.where(quarters == 0, 1.0, jnp.where(quarters == 2, -1.0, 0.0))
    by_sin = jnp.where(quarters == 1, 1.0, jnp.where(quarters == 3, -1.0, 0.0))
    fine_cos, fine_sin = small_ref[0, coarse:, :], small_ref[1, coarse:, :]
    fine_ref[0] = fine_cos * by_cos - fine_sin * by_sin
    fine_ref[1] = fine_sin * by_cos + fine_cos * by_sin

    def one(a, carry):
        big_cos = small_ref[0, pl.ds(a, 1), :]
        big_sin = small_ref[1, pl.ds(a, 1), :]
        start = pl.multiple_of(a * TABLE_STRIDE, TABLE_STRIDE)
        for part in range(0, TABLE_STRIDE, 16):
            fine_cos = fine_ref[0, part : part + 16, :]
            fine_sin = fine_ref[1, part : part + 16, :]
            rows = pl.ds(pl.multiple_of(start + part, 16), 16)
            out_ref[0, rows, :] = (big_cos * fine_cos - big_sin * fine_sin).astype(bf16)
            out_ref[1, rows, :] = (big_sin * fine_cos + big_cos * fine_sin).astype(bf16)
        return carry

    lax.fori_loop(0, coarse, one, 0)


VMEM = pl.BlockSpec(memory_space=pltpu.VMEM)
SMEM = pl.BlockSpec(memory_space=pltpu.SMEM)


def call(kernel, name, out_shape, operands, scalars=0, scratch=(), us=1.0):
    single = not isinstance(out_shape, (list, tuple))
    return pl.pallas_call(
        kernel,
        in_specs=[SMEM] * scalars + [VMEM] * (len(operands) - scalars),
        out_specs=VMEM if single else [VMEM] * len(out_shape),
        out_shape=out_shape,
        scratch_shapes=list(scratch),
        name=name,
        compiler_params=pltpu.CompilerParams(vmem_limit_bytes=16 * 1024 * 1024),
        cost_estimate=pl.CostEstimate(flops=int(us * FLOPS_US), bytes_accessed=0, transcendentals=0),
    )(*operands)


def block_start(blk_ref, bits, count):
    blk = blk_ref[0, 0]
    partner = (blk, blk + 1 - 2 * lax.rem(blk, 2), lax.rem(blk + 2, 4), 3 - blk)[bits]
    return pl.multiple_of(partner * count, count)


def fourier_table(blk, samples):
    shape = jax.ShapeDtypeStruct((2, MAXO, samples), bf16)
    small = jnp.asarray(small_tables(samples))
    return call(table_kernel, "table", shape, [blk, small], 1, [pltpu.VMEM((2, TABLE_STRIDE, samples), f32)])


def dot(a, b):
    return jnp.dot(a, b, preferred_element_type=f32)


def dot_t(a, b):
    return lax.dot_general(a, b, (((1,), (1,)), ((), ())), preferred_element_type=f32)


def exact_dot(a, b):
    return jnp.dot(a, b, preferred_element_type=f32, precision=lax.Precision.HIGHEST)


def levels_of(bucket_ref, points):
    point = lax.broadcasted_iota(jnp.int32, (points, 1), 0)
    level = jnp.zeros((points, 1), jnp.int32)
    for e in range(bucket_ref.shape[1]):
        value = jnp.int32(0)
        for position, orders in enumerate(bucket_orders):
            value = jnp.where(bucket_ref[0, e] == position, orders, value)
        level = jnp.where((point >= 25 * e) & (point < 25 * e + 25), value, level)
    return level


def arrange_kernel(blk_ref, bucket_hbm, disp_hbm, now_ref, *rest):
    *send_ref, disp_ref, bucket_ref, sems = rest
    points, _, count = disp_ref.shape
    buckets = pltpu.make_async_copy(bucket_hbm, bucket_ref, sems.at[0])
    field = pltpu.make_async_copy(disp_hbm, disp_ref, sems.at[1])
    buckets.start()
    field.start()
    now_ref[:, points:, :] = jnp.zeros((2, now_ref.shape[1] - points, count), f32)
    buckets.wait()
    order = lax.broadcasted_iota(jnp.int32, (points, count), 1) + blk_ref[0, 0] * count
    inside = order < levels_of(bucket_ref, points)
    field.wait()
    for c in range(2):
        kept = inside if c == 0 else inside & (order >= 1)
        now_ref[c, :points, :] = jnp.where(kept, disp_ref[:, c, :], 0.0)
    for i, s_ref in enumerate(send_ref):
        width = s_ref.shape[2]
        s_ref[...] = now_ref[:, :, i * width : (i + 1) * width].astype(bf16)


def arrange(blk, buckets, disp, pieces):
    shape = (2, PTS, disp.shape[2])
    sent = [jax.ShapeDtypeStruct((2, PTS, disp.shape[2] // pieces), bf16)] * pieces if pieces else []
    hbm = pl.BlockSpec(memory_space=pltpu.HBM)
    return pl.pallas_call(
        arrange_kernel,
        in_specs=[SMEM, hbm, hbm],
        out_specs=[VMEM] * (1 + pieces),
        out_shape=[jax.ShapeDtypeStruct(shape, f32), *sent],
        scratch_shapes=[
            pltpu.VMEM(disp.shape, f32),
            pltpu.SMEM(buckets.shape, jnp.int32),
            pltpu.SemaphoreType.DMA((2,)),
        ],
        name="arrange",
        compiler_params=pltpu.CompilerParams(vmem_limit_bytes=16 * 1024 * 1024),
    )(blk, buckets, disp)


def setup_kernel(bucket_ref, region_ref, radius_ref, weight_ref, column_ref, density_ref):
    points = radius_ref.shape[1]
    square = (points, points)
    diagonal = lax.broadcasted_iota(jnp.int32, square, 0) == lax.broadcasted_iota(jnp.int32, square, 1)
    radius = jnp.sum(jnp.where(diagonal, radius_ref[...], 0.0), axis=1, keepdims=True)
    weight = weight_ref[...] * radius
    column_ref[...] = jnp.zeros(column_ref.shape, f32)
    column_ref[:points, 0:1] = 1.0 / radius
    column_ref[:points, 1:2] = weight * (2.0 * math.pi / (2 * MAXO))
    column_ref[:points, 2:3] = levels_of(bucket_ref, points).astype(f32)
    column_ref[:points, 3:4] = time_step_sq / (weight * math.pi)
    shape = density_ref.shape
    row, lane = lax.broadcasted_iota(jnp.int32, shape, 0), lax.broadcasted_iota(jnp.int32, shape, 1)
    density = jnp.zeros(shape, f32)
    for e in range(region_ref.shape[1]):
        name = region_ref[0, e].astype(f32)
        density = jnp.where((row == ID_ROW) & (lane == e), name, density)
    density_ref[...] = density


def setup(buckets, regions, radius, weight, sectors):
    outs = [jax.ShapeDtypeStruct((PTS, 4), f32), jax.ShapeDtypeStruct((ELEM_ROWS, sectors), f32)]
    return call(setup_kernel, "setup", outs, [buckets, regions, radius, weight], 2)


def sides(mer_ref):
    here = 1 - lax.rem(mer_ref[0, 0], 2)
    return here, 1 - here


def coefficients_times_table(blk_ref, places, block_refs, table_ref):
    total = 0.0
    for (bits, piece), u_ref in zip(places, block_refs, strict=True):
        count = u_ref.shape[2]
        start = block_start(blk_ref, bits, MAXO // len(PARTNERS))
        start = pl.multiple_of(start + piece * count, count)
        order = (lax.broadcasted_iota(jnp.int32, (1, count), 1) + start).astype(f32)
        u0, u1 = u_ref[0], u_ref[1]
        cosine = jnp.concatenate([u0, (order * u1.astype(f32)).astype(bf16)])
        sine = jnp.concatenate([u1, (-order * u0.astype(f32)).astype(bf16)])
        total += dot(cosine, table_ref[0, pl.ds(start, count), :])
        total += dot(sine, table_ref[1, pl.ds(start, count), :])
    return total


def early_kernel(places, blk_ref, *refs):
    *block_refs, table_ref, phys_ref = refs
    phys_ref[...] = coefficients_times_table(blk_ref, places, block_refs, table_ref)


def early(blk, blocks, table):
    shape = jax.ShapeDtypeStruct((2 * PTS, table.shape[2]), f32)
    kernel = functools.partial(early_kernel, tuple(blocks))
    return call(kernel, "early", shape, [blk, *blocks.values(), table], 1, us=1.3)


def synthesis_kernel(section, places, blk_ref, mer_ref, nodes_ref, *refs):
    (
        *block_refs,
        phys_ref,
        kappa_ref,
        fwd_ref,
        table_ref,
        forward_ref,
        backward_ref,
        column_ref,
        sum_rows_ref,
        sum_cols_ref,
        before_ref,
        stress_ref,
        core_ref,
        chip_ref,
        density_ref,
        dens_ref,
        padded_ref,
    ) = refs
    points, samples = kappa_ref.shape
    inv_radius = column_ref[:, 0:1]
    quad = column_ref[:, 1:2]
    for i in range(4):
        padded_ref[i, PTS - 16 :, :] = jnp.zeros((16, samples), bf16)
        padded_ref[i, :points, :] = fwd_ref[section, i] if i < 3 else kappa_ref[...]
    phys = phys_ref[...] + coefficients_times_table(blk_ref, places, block_refs, table_ref)
    field, around = phys[:PTS], phys[PTS:] * inv_radius
    high = field.astype(bf16)
    low = (field - high.astype(f32)).astype(bf16)
    along = dot(forward_ref[...], jnp.concatenate([high, low, high]))
    along_s, along_z = along[:PTS], along[PTS:]
    modulus = padded_ref[3].astype(f32) * quad
    stress = jnp.concatenate([along_s * modulus, along_z * modulus]).astype(bf16)
    stress_ref[:PTS] = dot(backward_ref[...], jnp.concatenate([stress, stress]))
    stress_ref[PTS:] = around * modulus * inv_radius
    dens = (
        along_s * padded_ref[0].astype(f32)
        + along_z * padded_ref[1].astype(f32)
        + around * padded_ref[2].astype(f32)
    ) * (quad * kernel_scale)
    dens_high = dens.astype(bf16)
    dens_ref[:PTS] = dens_high
    dens_ref[PTS:] = (dens - dens_high.astype(f32)).astype(bf16)
    by_sector = dot(dens_ref[...], sum_cols_ref[...])
    density = before_ref[...] + exact_dot(sum_rows_ref[...], by_sector[:PTS] + by_sector[PTS:])
    density_ref[...] = density
    spare = jnp.zeros((8 - nodes_ref.shape[1], samples), f32)
    for o_ref, side in zip((core_ref, chip_ref), sides(mer_ref)):
        for part in range(2):
            rows = [stress_ref[pl.ds(PTS * part + nodes_ref[side, k], 1), :] for k in range(nodes_ref.shape[1])]
            o_ref[8 * part : 8 * part + 8, :] = jnp.concatenate([*rows, spare])


def synthesis(section, blk, mer, nodes, blocks, phys, kappa, fwd, table, consts, columns, before):
    forward, backward, sum_rows, sum_cols = consts
    samples = kappa.shape[1]
    outs = [
        jax.ShapeDtypeStruct((2 * PTS, samples), f32),
        jax.ShapeDtypeStruct((16, samples), f32),
        jax.ShapeDtypeStruct((16, samples), f32),
        jax.ShapeDtypeStruct(before.shape, f32),
    ]
    scratch = [
        pltpu.VMEM((2 * PTS, samples), bf16),
        pltpu.VMEM((4, PTS, samples), bf16),
    ]
    operands = [blk, mer, nodes, *blocks.values(), phys, kappa, fwd, table, forward, backward, columns, sum_rows, sum_cols, before]
    return call(functools.partial(synthesis_kernel, section, tuple(blocks)), "synthesis", outs, operands, 3, scratch, us=3.0)


def merge_kernel(mer_ref, nodes_ref, stress_ref, core_ref, chip_ref, out_ref, total_ref):
    total_ref[...] = stress_ref[...]
    for r_ref, side in zip((core_ref, chip_ref), sides(mer_ref)):
        rows = r_ref[...]
        for part in range(2):
            for k in range(nodes_ref.shape[1]):
                at = 8 * part + k
                total_ref[pl.ds(PTS * part + nodes_ref[side, k], 1), :] += rows[at : at + 1]
    out_ref[...] = total_ref[...].astype(bf16)


def merge(mer, nodes, stress, core, chip):
    shape = jax.ShapeDtypeStruct(stress.shape, bf16)
    scratch = [pltpu.VMEM(stress.shape, f32)]
    return call(merge_kernel, "merge", shape, [mer, nodes, stress, core, chip], 2, scratch, us=0.8)


def analysis_kernel(bits, piece, blk_ref, stress_ref, table_ref, o_ref):
    count = o_ref.shape[2]
    start = block_start(blk_ref, bits, MAXO // len(PARTNERS))
    start = pl.multiple_of(start + piece * count, count)
    order = (lax.broadcasted_iota(jnp.int32, (1, count), 1) + start).astype(f32)
    cosine = dot_t(stress_ref[...], table_ref[0, pl.ds(start, count), :])
    sine = dot_t(stress_ref[...], table_ref[1, pl.ds(start, count), :])
    o_ref[0] = (cosine[:PTS] - order * sine[PTS:]).astype(bf16)
    o_ref[1] = (sine[:PTS] + order * cosine[PTS:]).astype(bf16)


def analysis(bits, piece, blk, stress, table, count, us=0.75):
    shape = jax.ShapeDtypeStruct((2, PTS, count), bf16)
    kernel = functools.partial(analysis_kernel, bits, piece)
    return call(kernel, "analysis", shape, [blk, stress, table], 1, us=us)


def next_values(c, cols, total, parts, now, prev, column_ref, first_order):
    order = lax.broadcasted_iota(jnp.int32, now.shape, 1) + (first_order + cols.start)
    level = column_ref[:, 2:3]
    scale = column_ref[:, 3:4]
    gain = jnp.where(order == 0, scale * (0.5 if c == 0 else 0.0), scale)
    gain = jnp.where(order.astype(f32) < level, gain, 0.0)
    force = sum(p.astype(f32) for p in parts)
    return 2.0 * now - prev - gain * force


def update_kernel(piece, blk_ref, a_ref, b_ref, c_ref, d_ref, now_ref, prev_ref, column_ref, next_ref, send_ref):
    total, width = now_ref.shape[2], next_ref.shape[2]
    cols = slice(piece * width, (piece + 1) * width)
    for c in range(2):
        parts = [p[c] for p in (a_ref, b_ref, c_ref, d_ref)]
        now, prev = now_ref[c, :, cols], prev_ref[c, :, cols]
        value = next_values(c, cols, total, parts, now, prev, column_ref, blk_ref[0, 0] * total)
        next_ref[c] = value
        send_ref[c] = value.astype(bf16)


def update(piece, blk, parts, now, prev, columns):
    outs = [jax.ShapeDtypeStruct(parts[0].shape, f32), jax.ShapeDtypeStruct(parts[0].shape, bf16)]
    kernel = functools.partial(update_kernel, piece)
    return call(kernel, "update", outs, [blk, *parts, now, prev, columns], 1, us=0.3)


def finish_kernel(blk_ref, a_ref, b_ref, c_ref, d_ref, *refs):
    *now_refs, prev_ref, column_ref, out_ref = refs
    points, _, total = out_ref.shape
    width = now_refs[0].shape[2]
    for i, now_ref in enumerate(now_refs):
        cols = slice(i * width, (i + 1) * width)
        for c in range(2):
            parts = [p[c, :, cols] for p in (a_ref, b_ref, c_ref, d_ref)]
            prev = prev_ref[c, :, cols]
            value = next_values(c, cols, total, parts, now_ref[c], prev, column_ref, blk_ref[0, 0] * total)
            out_ref[:, c, cols] = value[:points]


def finish(blk, parts, now, prev, columns, points):
    shape = jax.ShapeDtypeStruct((points, 2, parts[0].shape[2]), f32)
    return call(finish_kernel, "finish", shape, [blk, *parts, *now, prev, columns], 1, us=1.2)


def join_kernel(*refs):
    rows = refs[0].shape[0]
    for i, ref in enumerate(refs[:-1]):
        refs[-1][i * rows : (i + 1) * rows] = ref[...]


def everywhere(x, piece):
    return {(bits, piece): swapped(x, "blk", bits) if bits else x for bits in PARTNERS}


def join(*pieces):
    shape = jax.ShapeDtypeStruct((len(pieces) * pieces[0].shape[0], pieces[0].shape[1]), f32)
    return call(join_kernel, "join", shape, pieces, us=0.35)


def joined(x, *bits):
    return join(x, *[swapped(x, "mer", b) for b in bits])


def owners_kernel(first_ref, *refs):
    *row_refs, out_ref = refs
    regions = out_ref.shape[0]
    total = jnp.zeros(out_ref.shape, f32)
    for rows_ref in row_refs:
        rows = rows_ref[...]
        count = rows.shape[0]
        names = rows[:, :128].reshape(count // ELEM_ROWS, ELEM_ROWS, 128)
        names = jnp.broadcast_to(names[:, ID_ROW : ID_ROW + 1], names.shape)
        element = lax.broadcasted_iota(jnp.int32, names.shape, 1)
        lane = lax.broadcasted_iota(jnp.int32, names.shape, 2)
        ids = jnp.sum(jnp.where((lane == element) & (element < ID_ROW), names, 0.0), axis=2, keepdims=True)
        ids = jnp.where(element[:, :, :1] < ID_ROW, ids, -1.0).reshape(count, 1)
        mine = (lax.broadcasted_iota(jnp.int32, (count, regions), 1) + first_ref[0, 0]).astype(f32)
        total = total + lax.dot_general(
            jnp.where(ids == mine, 1.0, 0.0),
            rows,
            (((0,), (0,)), ((), ())),
            preferred_element_type=f32,
            precision=lax.Precision.HIGHEST,
        )
    out_ref[...] = total


def owners(first, halves, regions):
    shape = jax.ShapeDtypeStruct((regions, halves[0].shape[1]), f32)
    return call(owners_kernel, "owners", shape, [first, *halves], 1, us=1.2)


def swapped(x, axis, bits):
    return lax.ppermute(x, axis, [(i, i ^ bits) for i in range(lax.axis_size(axis))])


def across_chips(x):
    ends = range(1, lax.axis_size("mer") - 1)
    return lax.ppermute(x, "mer", [(i, i + 1 if i % 2 else i - 1) for i in ends])


def tied(x, other):
    return lax.optimization_barrier((x, other))[0]


def local(disp_now, disp_prev, kappa, radius, fwd_strain, order_bucket, shared_nodes, region_map):
    points, _, count = disp_now.shape
    elements = order_bucket.shape[0]
    samp_count = kappa.shape[1]
    nphi = 2 * MAXO
    sectors = samp_count // 4
    regions = 4096 // lax.axis_size("mer")
    blk_index = lax.axis_index("blk").astype(jnp.int32)
    blk = blk_index.reshape(1, 1)
    mer = lax.axis_index("mer").astype(jnp.int32).reshape(1, 1)
    first = (lax.axis_index("mer").astype(jnp.int32) * regions).reshape(1, 1)
    buckets = order_bucket.reshape(1, -1)
    nodes = shared_nodes[0]
    in_hbm = lambda x: pltpu.with_memory_space_constraint(x, pltpu.HBM)
    buckets, disp_now, disp_prev = in_hbm(buckets), in_hbm(disp_now), in_hbm(disp_prev)
    current, send = arrange(blk, buckets, disp_now, 1)
    (previous,) = arrange(blk, buckets, disp_prev, 0)
    _, gllw = gll_tables()
    weight = jnp.asarray(np.tile(gllw, elements).reshape(-1, 1), f32)
    columns, density = setup(
        buckets, in_hbm(region_map.reshape(1, -1)), in_hbm(radius.reshape(1, -1)), in_hbm(weight), sectors
    )
    forward, backward = derivative_matrices(elements)
    sum_rows = np.zeros((ELEM_ROWS, PTS), np.float32)
    for e in range(elements):
        sum_rows[e, 25 * e : 25 * e + 25] = 1.0
    sum_cols = np.kron(np.eye(sectors), np.ones((4, 1))).astype(bf16)
    consts = tuple(jnp.asarray(x) for x in (forward, backward, sum_rows, sum_cols))
    blocks = everywhere(send, 0)
    fwd, columns, density, table_blk = lax.optimization_barrier((fwd_strain, columns, density, blk))
    table = fourier_table(table_blk, samp_count)

    late = {place: blocks.pop(place) for place in ((1, 0), (3, 0))}
    phys = early(blk, blocks, table)
    stress, core, chip, density = synthesis(
        0, blk, mer, nodes, late, phys, kappa, fwd, table, consts, columns, density
    )
    chip, core = across_chips(chip), swapped(core, "mer", 1)
    stress = merge(mer, nodes, stress, core, chip)
    pieces = range(PIECES)
    forces = [
        {bits: analysis(bits, h, blk, stress, table, count // len(pieces), us=0.05) for bits in (2, 1, 3, 0)}
        for h in pieces
    ]
    middle, blocks = [], []
    for h in pieces:
        parts = [forces[h][0]] + [swapped(forces[h][bits], "blk", bits) for bits in PARTNERS[1:]]
        following, send = update(h, blk, parts, current, previous, columns)
        middle.append(following)
        blocks.append(everywhere(send, h))

    stress, core, chip, density = synthesis(
        1, blk, mer, nodes, blocks[1], early(blk, blocks[0], table), kappa, fwd, table, consts, columns, density
    )
    chip, core = across_chips(chip), swapped(core, "mer", 1)
    gathered = swapped(density, "mer", 8)
    stress = merge(mer, nodes, stress, core, chip)
    forces = {2: analysis(2, 0, blk, stress, table, count)}
    gathered = join(tied(density, forces[2]), gathered)
    forces[1] = analysis(1, 0, blk, tied(stress, gathered), table, count)
    gathered = joined(gathered, 32)
    forces[3] = analysis(3, 0, blk, stress, table, count)
    gathered = tied(gathered, forces[3])
    forces[0] = analysis(0, 0, blk, tied(stress, gathered), table, count)
    gathered = joined(gathered, 16)
    parts = [forces[0]] + [swapped(forces[bits], "blk", bits) for bits in PARTNERS[1:]]
    gathered = joined(tied(gathered, [parts[1], parts[2], forces[0]]), 2, 4, 6)
    gathered = tied(gathered, parts[3])
    displacement = finish(blk, parts, middle, current, columns, points)
    return (displacement, owners(first, [gathered, swapped(gathered, "mer", 1)], regions))


def solution(mesh):
    in_specs = (
        P("mer", None, "blk"),
        P("mer", None, "blk"),
        P("mer", "blk"),
        P("mer"),
        P(None, None, "mer", "blk"),
        P("mer"),
        P("mer", None, None),
        P("mer"),
    )
    out_specs = (P("mer", None, "blk"), P("mer", "blk"))
    return jax.shard_map(local, mesh=mesh, in_specs=in_specs, out_specs=out_specs, check_vma=False)
```

```python
import functools
import math

import jax
import jax.numpy as jnp
import numpy as np
from jax import lax
from jax.experimental import pallas as pl
from jax.experimental.pallas import tpu as pltpu
from jax.sharding import PartitionSpec as P

MAXO = 2048
STEPS = 2
PIECES = 2
PTS = 128
ELEM_ROWS = 8
ID_ROW = 5
TABLE_STRIDE = 64
FLOPS_US = 1150000000
PARTNERS = (0, 2, 1, 3)

time_step_sq = 0.0004
kernel_scale = 0.0001
bucket_orders = (8, 64, 512, 2048)

f32 = jnp.float32
bf16 = jnp.bfloat16


def gll_tables():
    nodes = np.array([-1.0, -math.sqrt(3.0 / 7.0), 0.0, math.sqrt(3.0 / 7.0), 1.0])
    weights_line = np.array([0.1, 49.0 / 90.0, 32.0 / 45.0, 49.0 / 90.0, 0.1])
    legendre = (35.0 * nodes**4 - 30.0 * nodes**2 + 3.0) / 8.0
    deriv = np.zeros((5, 5))
    for row_index in range(5):
        for col_index in range(5):
            if row_index != col_index:
                deriv[row_index, col_index] = (
                    legendre[row_index]
                    / legendre[col_index]
                    / (nodes[row_index] - nodes[col_index])
                )
    deriv[0, 0] = -5.0
    deriv[4, 4] = 5.0
    return (deriv, np.outer(weights_line, weights_line).reshape(25))


def split_const(x):
    high = np.asarray(x, np.float32).astype(bf16)
    low = (np.asarray(x, np.float32) - high.astype(np.float32)).astype(bf16)
    return high, low


def derivative_matrices(elements):
    deriv, _ = gll_tables()
    along_s = np.zeros((PTS, PTS))
    along_z = np.zeros((PTS, PTS))
    for e in range(elements):
        base = slice(25 * e, 25 * e + 25)
        along_s[base, base] = np.kron(deriv, np.eye(5))
        along_z[base, base] = np.kron(np.eye(5), deriv)
    both = np.concatenate([along_s, along_z])
    high, low = split_const(both)
    forward = np.concatenate([high, high, low], axis=1)
    high_t, low_t = split_const(both.T)
    return forward, np.concatenate([high_t, low_t], axis=1)


def small_tables(samples):
    coarse = TABLE_STRIDE * np.arange(MAXO // TABLE_STRIDE)
    every = np.concatenate([coarse, np.arange(TABLE_STRIDE)])
    angle = (every[:, None] * np.arange(samples)[None, :] % (2 * MAXO)) * (math.pi / MAXO)
    return np.stack([np.cos(angle), np.sin(angle)]).astype(np.float32)


def table_kernel(blk_ref, small_ref, out_ref, fine_ref):
    coarse = MAXO // TABLE_STRIDE
    quarters = lax.broadcasted_iota(jnp.int32, (TABLE_STRIDE, 1), 0) * blk_ref[0, 0]
    quarters = jnp.bitwise_and(quarters, 3)
    by_cos = jnp.where(quarters == 0, 1.0, jnp.where(quarters == 2, -1.0, 0.0))
    by_sin = jnp.where(quarters == 1, 1.0, jnp.where(quarters == 3, -1.0, 0.0))
    fine_cos, fine_sin = small_ref[0, coarse:, :], small_ref[1, coarse:, :]
    fine_ref[0] = fine_cos * by_cos - fine_sin * by_sin
    fine_ref[1] = fine_sin * by_cos + fine_cos * by_sin

    def one(a, carry):
        big_cos = small_ref[0, pl.ds(a, 1), :]
        big_sin = small_ref[1, pl.ds(a, 1), :]
        start = pl.multiple_of(a * TABLE_STRIDE, TABLE_STRIDE)
        for part in range(0, TABLE_STRIDE, 16):
            fine_cos = fine_ref[0, part : part + 16, :]
            fine_sin = fine_ref[1, part : part + 16, :]
            rows = pl.ds(pl.multiple_of(start + part, 16), 16)
            out_ref[0, rows, :] = (big_cos * fine_cos - big_sin * fine_sin).astype(bf16)
            out_ref[1, rows, :] = (big_sin * fine_cos + big_cos * fine_sin).astype(bf16)
        return carry

    lax.fori_loop(0, coarse, one, 0)


VMEM = pl.BlockSpec(memory_space=pltpu.VMEM)
SMEM = pl.BlockSpec(memory_space=pltpu.SMEM)


def call(kernel, name, out_shape, operands, scalars=0, scratch=(), us=1.0):
    single = not isinstance(out_shape, (list, tuple))
    return pl.pallas_call(
        kernel,
        in_specs=[SMEM] * scalars + [VMEM] * (len(operands) - scalars),
        out_specs=VMEM if single else [VMEM] * len(out_shape),
        out_shape=out_shape,
        scratch_shapes=list(scratch),
        name=name,
        compiler_params=pltpu.CompilerParams(vmem_limit_bytes=16 * 1024 * 1024),
        cost_estimate=pl.CostEstimate(flops=int(us * FLOPS_US), bytes_accessed=0, transcendentals=0),
    )(*operands)


def block_start(blk_ref, bits, count):
    blk = blk_ref[0, 0]
    partner = (blk, blk + 1 - 2 * lax.rem(blk, 2), lax.rem(blk + 2, 4), 3 - blk)[bits]
    return pl.multiple_of(partner * count, count)


def fourier_table(blk, samples):
    shape = jax.ShapeDtypeStruct((2, MAXO, samples), bf16)
    small = jnp.asarray(small_tables(samples))
    return call(table_kernel, "table", shape, [blk, small], 1, [pltpu.VMEM((2, TABLE_STRIDE, samples), f32)])


def dot(a, b):
    return jnp.dot(a, b, preferred_element_type=f32)


def dot_t(a, b):
    return lax.dot_general(a, b, (((1,), (1,)), ((), ())), preferred_element_type=f32)


def exact_dot(a, b):
    return jnp.dot(a, b, preferred_element_type=f32, precision=lax.Precision.HIGHEST)


def levels_of(bucket_ref, points):
    point = lax.broadcasted_iota(jnp.int32, (points, 1), 0)
    level = jnp.zeros((points, 1), jnp.int32)
    for e in range(bucket_ref.shape[1]):
        value = jnp.int32(0)
        for position, orders in enumerate(bucket_orders):
            value = jnp.where(bucket_ref[0, e] == position, orders, value)
        level = jnp.where((point >= 25 * e) & (point < 25 * e + 25), value, level)
    return level


def arrange_kernel(blk_ref, bucket_hbm, disp_hbm, now_ref, *rest):
    *send_ref, disp_ref, bucket_ref, sems = rest
    points, _, count = disp_ref.shape
    buckets = pltpu.make_async_copy(bucket_hbm, bucket_ref, sems.at[0])
    field = pltpu.make_async_copy(disp_hbm, disp_ref, sems.at[1])
    buckets.start()
    field.start()
    now_ref[:, points:, :] = jnp.zeros((2, now_ref.shape[1] - points, count), f32)
    buckets.wait()
    order = lax.broadcasted_iota(jnp.int32, (points, count), 1) + blk_ref[0, 0] * count
    inside = order < levels_of(bucket_ref, points)
    field.wait()
    for c in range(2):
        kept = inside if c == 0 else inside & (order >= 1)
        now_ref[c, :points, :] = jnp.where(kept, disp_ref[:, c, :], 0.0)
    for i, s_ref in enumerate(send_ref):
        width = s_ref.shape[2]
        s_ref[...] = now_ref[:, :, i * width : (i + 1) * width].astype(bf16)


def arrange(blk, buckets, disp, pieces):
    shape = (2, PTS, disp.shape[2])
    sent = [jax.ShapeDtypeStruct((2, PTS, disp.shape[2] // pieces), bf16)] * pieces if pieces else []
    hbm = pl.BlockSpec(memory_space=pltpu.HBM)
    return pl.pallas_call(
        arrange_kernel,
        in_specs=[SMEM, hbm, hbm],
        out_specs=[VMEM] * (1 + pieces),
        out_shape=[jax.ShapeDtypeStruct(shape, f32), *sent],
        scratch_shapes=[
            pltpu.VMEM(disp.shape, f32),
            pltpu.SMEM(buckets.shape, jnp.int32),
            pltpu.SemaphoreType.DMA((2,)),
        ],
        name="arrange",
        compiler_params=pltpu.CompilerParams(vmem_limit_bytes=16 * 1024 * 1024),
    )(blk, buckets, disp)


def setup_kernel(bucket_ref, region_ref, radius_ref, weight_ref, column_ref, density_ref):
    points = radius_ref.shape[1]
    square = (points, points)
    diagonal = lax.broadcasted_iota(jnp.int32, square, 0) == lax.broadcasted_iota(jnp.int32, square, 1)
    radius = jnp.sum(jnp.where(diagonal, radius_ref[...], 0.0), axis=1, keepdims=True)
    weight = weight_ref[...] * radius
    column_ref[...] = jnp.zeros(column_ref.shape, f32)
    column_ref[:points, 0:1] = 1.0 / radius
    column_ref[:points, 1:2] = weight * (2.0 * math.pi / (2 * MAXO))
    column_ref[:points, 2:3] = levels_of(bucket_ref, points).astype(f32)
    column_ref[:points, 3:4] = time_step_sq / (weight * math.pi)
    shape = density_ref.shape
    row, lane = lax.broadcasted_iota(jnp.int32, shape, 0), lax.broadcasted_iota(jnp.int32, shape, 1)
    density = jnp.zeros(shape, f32)
    for e in range(region_ref.shape[1]):
        name = region_ref[0, e].astype(f32)
        density = jnp.where((row == ID_ROW) & (lane == e), name, density)
    density_ref[...] = density


def setup(buckets, regions, radius, weight, sectors):
    outs = [jax.ShapeDtypeStruct((PTS, 4), f32), jax.ShapeDtypeStruct((ELEM_ROWS, sectors), f32)]
    return call(setup_kernel, "setup", outs, [buckets, regions, radius, weight], 2)


def sides(mer_ref):
    here = 1 - lax.rem(mer_ref[0, 0], 2)
    return here, 1 - here


def coefficients_times_table(blk_ref, places, block_refs, table_ref):
    total = 0.0
    for (bits, piece), u_ref in zip(places, block_refs, strict=True):
        count = u_ref.shape[2]
        start = block_start(blk_ref, bits, MAXO // len(PARTNERS))
        start = pl.multiple_of(start + piece * count, count)
        order = (lax.broadcasted_iota(jnp.int32, (1, count), 1) + start).astype(f32)
        u0, u1 = u_ref[0], u_ref[1]
        cosine = jnp.concatenate([u0, (order * u1.astype(f32)).astype(bf16)])
        sine = jnp.concatenate([u1, (-order * u0.astype(f32)).astype(bf16)])
        total += dot(cosine, table_ref[0, pl.ds(start, count), :])
        total += dot(sine, table_ref[1, pl.ds(start, count), :])
    return total


def copy_rows(mer_ref, nodes_ref, row, out_refs):
    for o_ref, side in zip(out_refs, sides(mer_ref)):
        for part in range(2):
            rows = [row(part, nodes_ref[side, k]) for k in range(nodes_ref.shape[1])]
            rows.append(jnp.zeros((8 - len(rows), o_ref.shape[1]), f32))
            o_ref[8 * part : 8 * part + 8, :] = jnp.concatenate(rows)


def early_kernel(places, blk_ref, *refs):
    *block_refs, table_ref, phys_ref = refs
    phys_ref[...] = coefficients_times_table(blk_ref, places, block_refs, table_ref)


def early(blk, blocks, table):
    shape = jax.ShapeDtypeStruct((2 * PTS, table.shape[2]), f32)
    kernel = functools.partial(early_kernel, tuple(blocks))
    return call(kernel, "early", shape, [blk, *blocks.values(), table], 1, us=1.3)


def synthesis_kernel(section, places, blk_ref, mer_ref, nodes_ref, *refs):
    block_refs = refs[: len(places)]
    (
        phys_ref,
        kappa_ref,
        fwd_ref,
        table_ref,
        forward_ref,
        backward_ref,
        column_ref,
        sum_rows_ref,
        sum_cols_ref,
        before_ref,
        stress_ref,
        density_ref,
        *row_refs,
        dens_ref,
        padded_ref,
    ) = refs[len(places) :]
    points, samples = kappa_ref.shape
    inv_radius = column_ref[:, 0:1]
    quad = column_ref[:, 1:2]
    for i in range(4):
        padded_ref[i, PTS - 16 :, :] = jnp.zeros((16, samples), bf16)
        padded_ref[i, :points, :] = fwd_ref[section, i] if i < 3 else kappa_ref[...]
    phys = phys_ref[...] + coefficients_times_table(blk_ref, places, block_refs, table_ref)
    field, around = phys[:PTS], phys[PTS:] * inv_radius
    high = field.astype(bf16)
    low = (field - high.astype(f32)).astype(bf16)
    along = dot(forward_ref[...], jnp.concatenate([high, low, high]))
    along_s, along_z = along[:PTS], along[PTS:]
    modulus = padded_ref[3].astype(f32) * quad
    stress = jnp.concatenate([along_s * modulus, along_z * modulus]).astype(bf16)
    stress_ref[:PTS] = dot(backward_ref[...], jnp.concatenate([stress, stress])).astype(stress_ref.dtype)
    stress_ref[PTS:] = (around * modulus * inv_radius).astype(stress_ref.dtype)
    dens = (
        along_s * padded_ref[0].astype(f32)
        + along_z * padded_ref[1].astype(f32)
        + around * padded_ref[2].astype(f32)
    ) * (quad * kernel_scale)
    dens_high = dens.astype(bf16)
    dens_ref[:PTS] = dens_high
    dens_ref[PTS:] = (dens - dens_high.astype(f32)).astype(bf16)
    by_sector = dot(dens_ref[...], sum_cols_ref[...])
    density_ref[...] = before_ref[...] + exact_dot(sum_rows_ref[...], by_sector[:PTS] + by_sector[PTS:])
    if row_refs:
        copy_rows(mer_ref, nodes_ref, lambda part, at: stress_ref[pl.ds(PTS * part + at, 1), :], row_refs)


def synthesis(section, blk, mer, nodes, blocks, phys, kappa, fwd, table, consts, columns, before):
    forward, backward, sum_rows, sum_cols = consts
    samples = kappa.shape[1]
    last = section == STEPS - 1
    outs = [
        jax.ShapeDtypeStruct((2 * PTS, samples), bf16 if last else f32),
        jax.ShapeDtypeStruct(before.shape, f32),
    ]
    if not last:
        outs += [jax.ShapeDtypeStruct((16, samples), f32)] * 2
    scratch = [
        pltpu.VMEM((2 * PTS, samples), bf16),
        pltpu.VMEM((4, PTS, samples), bf16),
    ]
    operands = [blk, mer, nodes, *blocks.values(), phys, kappa, fwd, table, forward, backward, columns, sum_rows, sum_cols, before]
    return call(functools.partial(synthesis_kernel, section, tuple(blocks)), "synthesis", outs, operands, 3, scratch, us=3.0)


def merge_kernel(mer_ref, nodes_ref, stress_ref, core_ref, chip_ref, out_ref, total_ref):
    total_ref[...] = stress_ref[...]
    for r_ref, side in zip((core_ref, chip_ref), sides(mer_ref)):
        rows = r_ref[...]
        for part in range(2):
            for k in range(nodes_ref.shape[1]):
                at = 8 * part + k
                total_ref[pl.ds(PTS * part + nodes_ref[side, k], 1), :] += rows[at : at + 1]
    out_ref[...] = total_ref[...].astype(bf16)


def merge(mer, nodes, stress, core, chip):
    shape = jax.ShapeDtypeStruct(stress.shape, bf16)
    scratch = [pltpu.VMEM(stress.shape, f32)]
    return call(merge_kernel, "merge", shape, [mer, nodes, stress, core, chip], 2, scratch, us=0.8)


def analysis_kernel(bits, piece, blk_ref, stress_ref, table_ref, o_ref):
    count = o_ref.shape[2]
    start = block_start(blk_ref, bits, MAXO // len(PARTNERS))
    start = pl.multiple_of(start + piece * count, count)
    order = (lax.broadcasted_iota(jnp.int32, (1, count), 1) + start).astype(f32)
    cosine = dot_t(stress_ref[...], table_ref[0, pl.ds(start, count), :])
    sine = dot_t(stress_ref[...], table_ref[1, pl.ds(start, count), :])
    o_ref[0] = (cosine[:PTS] - order * sine[PTS:]).astype(bf16)
    o_ref[1] = (sine[:PTS] + order * cosine[PTS:]).astype(bf16)


def analysis(bits, piece, blk, stress, table, count, us=0.75):
    shape = jax.ShapeDtypeStruct((2, PTS, count), bf16)
    kernel = functools.partial(analysis_kernel, bits, piece)
    return call(kernel, "analysis", shape, [blk, stress, table], 1, us=us)


def next_values(c, cols, total, parts, now, prev, column_ref, first_order):
    order = lax.broadcasted_iota(jnp.int32, now.shape, 1) + (first_order + cols.start)
    level = column_ref[:, 2:3]
    scale = column_ref[:, 3:4]
    gain = jnp.where(order == 0, scale * (0.5 if c == 0 else 0.0), scale)
    gain = jnp.where(order.astype(f32) < level, gain, 0.0)
    force = sum(p.astype(f32) for p in parts)
    return 2.0 * now - prev - gain * force


def update_kernel(piece, blk_ref, a_ref, b_ref, c_ref, d_ref, now_ref, prev_ref, column_ref, next_ref, send_ref):
    total, width = now_ref.shape[2], next_ref.shape[2]
    cols = slice(piece * width, (piece + 1) * width)
    for c in range(2):
        parts = [p[c] for p in (a_ref, b_ref, c_ref, d_ref)]
        now, prev = now_ref[c, :, cols], prev_ref[c, :, cols]
        value = next_values(c, cols, total, parts, now, prev, column_ref, blk_ref[0, 0] * total)
        next_ref[c] = value
        send_ref[c] = value.astype(bf16)


def update(piece, blk, parts, now, prev, columns):
    outs = [jax.ShapeDtypeStruct(parts[0].shape, f32), jax.ShapeDtypeStruct(parts[0].shape, bf16)]
    kernel = functools.partial(update_kernel, piece)
    return call(kernel, "update", outs, [blk, *parts, now, prev, columns], 1, us=0.3)


def shared_kernel(mer_ref, nodes_ref, a_ref, b_ref, c_ref, d_ref, total_ref, core_ref, chip_ref):
    for c in range(2):
        total_ref[c] = sum(p[c].astype(f32) for p in (a_ref, b_ref, c_ref, d_ref))
    copy_rows(mer_ref, nodes_ref, lambda c, at: total_ref[c, pl.ds(at, 1), :], (core_ref, chip_ref))


def shared(mer, nodes, parts):
    rows = jax.ShapeDtypeStruct((16, parts[0].shape[2]), f32)
    outs = [jax.ShapeDtypeStruct(parts[0].shape, f32), rows, rows]
    return call(shared_kernel, "shared", outs, [mer, nodes, *parts], 2, us=0.5)


def finish_kernel(blk_ref, mer_ref, nodes_ref, force_ref, core_ref, chip_ref, *refs):
    *now_refs, prev_ref, column_ref, out_ref, total_ref = refs
    total_ref[...] = force_ref[...]
    for r_ref, side in zip((core_ref, chip_ref), sides(mer_ref)):
        rows = r_ref[...]
        for c in range(2):
            for k in range(nodes_ref.shape[1]):
                at = 8 * c + k
                total_ref[c, pl.ds(nodes_ref[side, k], 1), :] += rows[at : at + 1]
    points, _, total = out_ref.shape
    width = now_refs[0].shape[2]
    for i, now_ref in enumerate(now_refs):
        cols = slice(i * width, (i + 1) * width)
        for c in range(2):
            force, prev = total_ref[c, :, cols], prev_ref[c, :, cols]
            value = next_values(c, cols, total, [force], now_ref[c], prev, column_ref, blk_ref[0, 0] * total)
            out_ref[:, c, cols] = value[:points]


def finish(blk, mer, nodes, force, core, chip, now, prev, columns, points):
    shape = jax.ShapeDtypeStruct((points, 2, force.shape[2]), f32)
    operands = [blk, mer, nodes, force, core, chip, *now, prev, columns]
    return call(finish_kernel, "finish", shape, operands, 3, [pltpu.VMEM(force.shape, f32)], us=1.3)


def join_kernel(*refs):
    rows = refs[0].shape[0]
    for i, ref in enumerate(refs[:-1]):
        refs[-1][i * rows : (i + 1) * rows] = ref[...]


def everywhere(x, piece):
    return {(bits, piece): swapped(x, "blk", bits) if bits else x for bits in PARTNERS}


def join(*pieces):
    shape = jax.ShapeDtypeStruct((len(pieces) * pieces[0].shape[0], pieces[0].shape[1]), f32)
    return call(join_kernel, "join", shape, pieces, us=0.35)


def joined(x, *bits):
    return join(x, *[swapped(x, "mer", b) for b in bits])


def owners_kernel(first_ref, rows_ref, before_ref, out_ref):
    regions = out_ref.shape[0]
    rows = rows_ref[...]
    count = rows.shape[0]
    names = rows[:, :128].reshape(count // ELEM_ROWS, ELEM_ROWS, 128)
    names = jnp.broadcast_to(names[:, ID_ROW : ID_ROW + 1], names.shape)
    element = lax.broadcasted_iota(jnp.int32, names.shape, 1)
    lane = lax.broadcasted_iota(jnp.int32, names.shape, 2)
    ids = jnp.sum(jnp.where((lane == element) & (element < ID_ROW), names, 0.0), axis=2, keepdims=True)
    ids = jnp.where(element[:, :, :1] < ID_ROW, ids, -1.0).reshape(count, 1)
    mine = (lax.broadcasted_iota(jnp.int32, (count, regions), 1) + first_ref[0, 0]).astype(f32)
    out_ref[...] = before_ref[...] + lax.dot_general(
        jnp.where(ids == mine, 1.0, 0.0),
        rows,
        (((0,), (0,)), ((), ())),
        preferred_element_type=f32,
        precision=lax.Precision.HIGHEST,
    )


def owners(first, rows, before):
    shape = jax.ShapeDtypeStruct(before.shape, f32)
    return call(owners_kernel, "owners", shape, [first, rows, before], 1, us=0.8)


def swapped(x, axis, bits):
    return lax.ppermute(x, axis, [(i, i ^ bits) for i in range(lax.axis_size(axis))])


def across_chips(x):
    ends = range(1, lax.axis_size("mer") - 1)
    return lax.ppermute(x, "mer", [(i, i + 1 if i % 2 else i - 1) for i in ends])


def tied(x, other):
    return lax.optimization_barrier((x, other))[0]


def local(disp_now, disp_prev, kappa, radius, fwd_strain, order_bucket, shared_nodes, region_map):
    points, _, count = disp_now.shape
    elements = order_bucket.shape[0]
    samp_count = kappa.shape[1]
    nphi = 2 * MAXO
    sectors = samp_count // 4
    regions = 4096 // lax.axis_size("mer")
    blk_index = lax.axis_index("blk").astype(jnp.int32)
    blk = blk_index.reshape(1, 1)
    mer = lax.axis_index("mer").astype(jnp.int32).reshape(1, 1)
    first = (lax.axis_index("mer").astype(jnp.int32) * regions).reshape(1, 1)
    buckets = order_bucket.reshape(1, -1)
    nodes = shared_nodes[0]
    in_hbm = lambda x: pltpu.with_memory_space_constraint(x, pltpu.HBM)
    buckets, disp_now, disp_prev = in_hbm(buckets), in_hbm(disp_now), in_hbm(disp_prev)
    current, send = arrange(blk, buckets, disp_now, 1)
    (previous,) = arrange(blk, buckets, disp_prev, 0)
    _, gllw = gll_tables()
    weight = jnp.asarray(np.tile(gllw, elements).reshape(-1, 1), f32)
    columns, density = setup(
        buckets, in_hbm(region_map.reshape(1, -1)), in_hbm(radius.reshape(1, -1)), in_hbm(weight), sectors
    )
    forward, backward = derivative_matrices(elements)
    sum_rows = np.zeros((ELEM_ROWS, PTS), np.float32)
    for e in range(elements):
        sum_rows[e, 25 * e : 25 * e + 25] = 1.0
    sum_cols = np.kron(np.eye(sectors), np.ones((4, 1))).astype(bf16)
    consts = tuple(jnp.asarray(x) for x in (forward, backward, sum_rows, sum_cols))
    blocks = everywhere(send, 0)
    fwd, columns, density, table_blk = lax.optimization_barrier((fwd_strain, columns, density, blk))
    table = fourier_table(table_blk, samp_count)

    late = {place: blocks.pop(place) for place in ((1, 0), (3, 0))}
    phys = tied(early(blk, blocks, table), previous)
    stress, density, core, chip = synthesis(
        0, blk, mer, nodes, late, phys, kappa, fwd, table, consts, columns, density
    )
    chip, core = across_chips(chip), swapped(core, "mer", 1)
    stress = merge(mer, nodes, stress, core, chip)
    pieces = range(PIECES)
    forces = [
        {bits: analysis(bits, h, blk, stress, table, count // len(pieces), us=0.05) for bits in (2, 1, 3, 0)}
        for h in pieces
    ]
    middle, blocks = [], []
    for h in pieces:
        sent = [forces[h][bits] for bits in PARTNERS]
        parts = [swapped(x, "blk", bits) if bits else x for x, bits in zip(sent, PARTNERS)]
        following, send = update(h, blk, parts, current, previous, columns)
        middle.append(following)
        blocks.append(everywhere(send, h))

    stress, density = synthesis(
        1, blk, mer, nodes, blocks[1], early(blk, blocks[0], table), kappa, fwd, table, consts, columns, density
    )
    gathered = swapped(density, "mer", 8)
    forces = {bits: analysis(bits, 0, blk, stress, table, count) for bits in (2, 1)}
    gathered = join(tied(density, forces[2]), gathered)
    forces[3] = analysis(3, 0, blk, tied(stress, gathered), table, count)
    gathered = joined(tied(gathered, [forces[1], forces[3]]), 56)
    forces[0] = analysis(0, 0, blk, stress, table, count)
    parts = [swapped(forces[bits], "blk", bits) if bits else forces[0] for bits in PARTNERS]
    gathered = joined(tied(gathered, [parts[1], forces[0]]), 16)
    force, core, chip = shared(mer, nodes, parts)
    chip, core = across_chips(chip), swapped(core, "mer", 1)
    gathered = tied(gathered, force)
    near = [swapped(gathered, "mer", bits) for bits in (4, 2)]
    gathered = join(gathered, *near, swapped(tied(gathered, [chip, core]), "mer", 6))
    displacement = finish(blk, mer, nodes, force, core, chip, middle, current, columns, points)
    kernel = owners(first, gathered, jnp.zeros((regions, sectors), f32))
    return (displacement, owners(first, swapped(gathered, "mer", 1), kernel))


def solution(mesh):
    in_specs = (
        P("mer", None, "blk"),
        P("mer", None, "blk"),
        P("mer", "blk"),
        P("mer"),
        P(None, None, "mer", "blk"),
        P("mer"),
        P("mer", None, None),
        P("mer"),
    )
    out_specs = (P("mer", None, "blk"), P("mer", "blk"))
    return jax.shard_map(local, mesh=mesh, in_specs=in_specs, out_specs=out_specs, check_vma=False)
```

```python
import functools
import math

import jax
import jax.numpy as jnp
import numpy as np
from jax import lax
from jax.experimental import pallas as pl
from jax.experimental.pallas import tpu as pltpu
from jax.sharding import PartitionSpec as P

MAXO = 2048
STEPS = 2
PIECES = 2
PTS = 128
ELEM_ROWS = 8
ID_ROW = 5
TABLE_STRIDE = 64
FLOPS_US = 3450000000
PARTNERS = (0, 2, 1, 3)

time_step_sq = 0.0004
kernel_scale = 0.0001
bucket_orders = (8, 64, 512, 2048)

f32 = jnp.float32
bf16 = jnp.bfloat16


def gll_tables():
    nodes = np.array([-1.0, -math.sqrt(3.0 / 7.0), 0.0, math.sqrt(3.0 / 7.0), 1.0])
    weights_line = np.array([0.1, 49.0 / 90.0, 32.0 / 45.0, 49.0 / 90.0, 0.1])
    legendre = (35.0 * nodes**4 - 30.0 * nodes**2 + 3.0) / 8.0
    deriv = np.zeros((5, 5))
    for row_index in range(5):
        for col_index in range(5):
            if row_index != col_index:
                deriv[row_index, col_index] = (
                    legendre[row_index]
                    / legendre[col_index]
                    / (nodes[row_index] - nodes[col_index])
                )
    deriv[0, 0] = -5.0
    deriv[4, 4] = 5.0
    return (deriv, np.outer(weights_line, weights_line).reshape(25))


def split_const(x):
    high = np.asarray(x, np.float32).astype(bf16)
    low = (np.asarray(x, np.float32) - high.astype(np.float32)).astype(bf16)
    return high, low


def derivative_matrices(elements):
    deriv, _ = gll_tables()
    along_s = np.zeros((PTS, PTS))
    along_z = np.zeros((PTS, PTS))
    for e in range(elements):
        base = slice(25 * e, 25 * e + 25)
        along_s[base, base] = np.kron(deriv, np.eye(5))
        along_z[base, base] = np.kron(np.eye(5), deriv)
    both = np.concatenate([along_s, along_z])
    high, low = split_const(both)
    forward = np.concatenate([high, high, low], axis=1)
    high_t, low_t = split_const(both.T)
    return forward, np.concatenate([high_t, low_t], axis=1)


def small_tables(samples):
    coarse = TABLE_STRIDE * np.arange(MAXO // TABLE_STRIDE)
    every = np.concatenate([coarse, np.arange(TABLE_STRIDE)])
    angle = (every[:, None] * np.arange(samples)[None, :] % (2 * MAXO)) * (math.pi / MAXO)
    return np.stack([np.cos(angle), np.sin(angle)]).astype(np.float32)


def table_kernel(blk_ref, small_ref, out_ref, fine_ref):
    coarse = MAXO // TABLE_STRIDE
    quarters = lax.broadcasted_iota(jnp.int32, (TABLE_STRIDE, 1), 0) * blk_ref[0, 0]
    quarters = jnp.bitwise_and(quarters, 3)
    by_cos = jnp.where(quarters == 0, 1.0, jnp.where(quarters == 2, -1.0, 0.0))
    by_sin = jnp.where(quarters == 1, 1.0, jnp.where(quarters == 3, -1.0, 0.0))
    fine_cos, fine_sin = small_ref[0, coarse:, :], small_ref[1, coarse:, :]
    fine_ref[0] = fine_cos * by_cos - fine_sin * by_sin
    fine_ref[1] = fine_sin * by_cos + fine_cos * by_sin

    def one(a, carry):
        big_cos = small_ref[0, pl.ds(a, 1), :]
        big_sin = small_ref[1, pl.ds(a, 1), :]
        start = pl.multiple_of(a * TABLE_STRIDE, TABLE_STRIDE)
        for part in range(0, TABLE_STRIDE, 16):
            fine_cos = fine_ref[0, part : part + 16, :]
            fine_sin = fine_ref[1, part : part + 16, :]
            rows = pl.ds(pl.multiple_of(start + part, 16), 16)
            out_ref[0, rows, :] = (big_cos * fine_cos - big_sin * fine_sin).astype(bf16)
            out_ref[1, rows, :] = (big_sin * fine_cos + big_cos * fine_sin).astype(bf16)
        return carry

    lax.fori_loop(0, coarse, one, 0)


VMEM = pl.BlockSpec(memory_space=pltpu.VMEM)
SMEM = pl.BlockSpec(memory_space=pltpu.SMEM)


def call(kernel, name, out_shape, operands, scalars=0, scratch=(), us=1.0):
    single = not isinstance(out_shape, (list, tuple))
    return pl.pallas_call(
        kernel,
        in_specs=[SMEM] * scalars + [VMEM] * (len(operands) - scalars),
        out_specs=VMEM if single else [VMEM] * len(out_shape),
        out_shape=out_shape,
        scratch_shapes=list(scratch),
        name=name,
        compiler_params=pltpu.CompilerParams(vmem_limit_bytes=16 * 1024 * 1024),
        cost_estimate=pl.CostEstimate(flops=int(us * FLOPS_US), bytes_accessed=0, transcendentals=0),
    )(*operands)


def block_start(blk_ref, bits, count):
    blk = blk_ref[0, 0]
    partner = (blk, blk + 1 - 2 * lax.rem(blk, 2), lax.rem(blk + 2, 4), 3 - blk)[bits]
    return pl.multiple_of(partner * count, count)


def fourier_table(blk, samples):
    shape = jax.ShapeDtypeStruct((2, MAXO, samples), bf16)
    small = jnp.asarray(small_tables(samples))
    return call(table_kernel, "table", shape, [blk, small], 1, [pltpu.VMEM((2, TABLE_STRIDE, samples), f32)])


def dot(a, b):
    return jnp.dot(a, b, preferred_element_type=f32)


def dot_t(a, b):
    return lax.dot_general(a, b, (((1,), (1,)), ((), ())), preferred_element_type=f32)


def exact_dot(a, b):
    return jnp.dot(a, b, preferred_element_type=f32, precision=lax.Precision.HIGHEST)


def levels_of(bucket_ref, points):
    point = lax.broadcasted_iota(jnp.int32, (points, 1), 0)
    level = jnp.zeros((points, 1), jnp.int32)
    for e in range(bucket_ref.shape[1]):
        value = jnp.int32(0)
        for position, orders in enumerate(bucket_orders):
            value = jnp.where(bucket_ref[0, e] == position, orders, value)
        level = jnp.where((point >= 25 * e) & (point < 25 * e + 25), value, level)
    return level


def arrange_kernel(blk_ref, bucket_hbm, disp_hbm, now_ref, *rest):
    *send_ref, disp_ref, bucket_ref, sems = rest
    points, _, count = disp_ref.shape
    buckets = pltpu.make_async_copy(bucket_hbm, bucket_ref, sems.at[0])
    field = pltpu.make_async_copy(disp_hbm, disp_ref, sems.at[1])
    buckets.start()
    field.start()
    now_ref[:, points:, :] = jnp.zeros((2, now_ref.shape[1] - points, count), f32)
    buckets.wait()
    order = lax.broadcasted_iota(jnp.int32, (points, count), 1) + blk_ref[0, 0] * count
    inside = order < levels_of(bucket_ref, points)
    field.wait()
    for c in range(2):
        kept = inside if c == 0 else inside & (order >= 1)
        now_ref[c, :points, :] = jnp.where(kept, disp_ref[:, c, :], 0.0)
    for i, s_ref in enumerate(send_ref):
        width = s_ref.shape[2]
        s_ref[...] = now_ref[:, :, i * width : (i + 1) * width].astype(bf16)


def arrange(blk, buckets, disp, pieces):
    shape = (2, PTS, disp.shape[2])
    sent = [jax.ShapeDtypeStruct((2, PTS, disp.shape[2] // pieces), bf16)] * pieces if pieces else []
    hbm = pl.BlockSpec(memory_space=pltpu.HBM)
    return pl.pallas_call(
        arrange_kernel,
        in_specs=[SMEM, hbm, hbm],
        out_specs=[VMEM] * (1 + pieces),
        out_shape=[jax.ShapeDtypeStruct(shape, f32), *sent],
        scratch_shapes=[
            pltpu.VMEM(disp.shape, f32),
            pltpu.SMEM(buckets.shape, jnp.int32),
            pltpu.SemaphoreType.DMA((2,)),
        ],
        name="arrange",
        compiler_params=pltpu.CompilerParams(vmem_limit_bytes=16 * 1024 * 1024),
    )(blk, buckets, disp)


def setup_kernel(bucket_ref, region_ref, radius_ref, weight_ref, column_ref, density_ref):
    points = radius_ref.shape[1]
    square = (points, points)
    diagonal = lax.broadcasted_iota(jnp.int32, square, 0) == lax.broadcasted_iota(jnp.int32, square, 1)
    radius = jnp.sum(jnp.where(diagonal, radius_ref[...], 0.0), axis=1, keepdims=True)
    weight = weight_ref[...] * radius
    column_ref[...] = jnp.zeros(column_ref.shape, f32)
    column_ref[:points, 0:1] = 1.0 / radius
    column_ref[:points, 1:2] = weight * (2.0 * math.pi / (2 * MAXO))
    column_ref[:points, 2:3] = levels_of(bucket_ref, points).astype(f32)
    column_ref[:points, 3:4] = time_step_sq / (weight * math.pi)
    shape = density_ref.shape
    row, lane = lax.broadcasted_iota(jnp.int32, shape, 0), lax.broadcasted_iota(jnp.int32, shape, 1)
    density = jnp.zeros(shape, f32)
    for e in range(region_ref.shape[1]):
        name = region_ref[0, e].astype(f32)
        density = jnp.where((row == ID_ROW) & (lane == e), name, density)
    density_ref[...] = density


def setup(buckets, regions, radius, weight, sectors):
    outs = [jax.ShapeDtypeStruct((PTS, 4), f32), jax.ShapeDtypeStruct((ELEM_ROWS, sectors), f32)]
    return call(setup_kernel, "setup", outs, [buckets, regions, radius, weight], 2)


def sides(mer_ref):
    here = 1 - lax.rem(mer_ref[0, 0], 2)
    return here, 1 - here


def coefficients_times_table(blk_ref, places, block_refs, table_ref):
    total = 0.0
    for (bits, piece), u_ref in zip(places, block_refs, strict=True):
        count = u_ref.shape[2]
        start = block_start(blk_ref, bits, MAXO // len(PARTNERS))
        start = pl.multiple_of(start + piece * count, count)
        order = (lax.broadcasted_iota(jnp.int32, (1, count), 1) + start).astype(f32)
        u0, u1 = u_ref[0], u_ref[1]
        cosine = jnp.concatenate([u0, (order * u1.astype(f32)).astype(bf16)])
        sine = jnp.concatenate([u1, (-order * u0.astype(f32)).astype(bf16)])
        total += dot(cosine, table_ref[0, pl.ds(start, count), :])
        total += dot(sine, table_ref[1, pl.ds(start, count), :])
    return total


def copy_rows(mer_ref, nodes_ref, row, out_refs):
    for o_ref, side in zip(out_refs, sides(mer_ref)):
        rows = []
        for part in range(2):
            rows += [row(part, nodes_ref[side, k]) for k in range(nodes_ref.shape[1])]
            rows.append(jnp.zeros((8 - nodes_ref.shape[1], o_ref.shape[1]), f32))
        o_ref[...] = jnp.concatenate(rows).astype(o_ref.dtype)


def early_kernel(places, blk_ref, *refs):
    *block_refs, table_ref, phys_ref = refs
    phys_ref[...] = coefficients_times_table(blk_ref, places, block_refs, table_ref)


def early(blk, blocks, table):
    shape = jax.ShapeDtypeStruct((2 * PTS, table.shape[2]), f32)
    kernel = functools.partial(early_kernel, tuple(blocks))
    return call(kernel, "early", shape, [blk, *blocks.values(), table], 1, us=1.3)


def synthesis_kernel(section, places, blk_ref, mer_ref, nodes_ref, *refs):
    block_refs = refs[: len(places)]
    (
        phys_ref,
        kappa_ref,
        fwd_ref,
        table_ref,
        forward_ref,
        backward_ref,
        column_ref,
        sum_rows_ref,
        sum_cols_ref,
        before_ref,
        stress_ref,
        density_ref,
        *row_refs,
        dens_ref,
        padded_ref,
    ) = refs[len(places) :]
    points, samples = kappa_ref.shape
    inv_radius = column_ref[:, 0:1]
    quad = column_ref[:, 1:2]
    for i in range(4):
        padded_ref[i, PTS - 16 :, :] = jnp.zeros((16, samples), bf16)
        padded_ref[i, :points, :] = fwd_ref[section, i] if i < 3 else kappa_ref[...]
    phys = phys_ref[...] + coefficients_times_table(blk_ref, places, block_refs, table_ref)
    field, around = phys[:PTS], phys[PTS:] * inv_radius
    high = field.astype(bf16)
    low = (field - high.astype(f32)).astype(bf16)
    along = dot(forward_ref[...], jnp.concatenate([high, low, high]))
    along_s, along_z = along[:PTS], along[PTS:]
    modulus = padded_ref[3].astype(f32) * quad
    stress = jnp.concatenate([along_s * modulus, along_z * modulus]).astype(bf16)
    stress_ref[:PTS] = dot(backward_ref[...], jnp.concatenate([stress, stress])).astype(stress_ref.dtype)
    stress_ref[PTS:] = (around * modulus * inv_radius).astype(stress_ref.dtype)
    dens = (
        along_s * padded_ref[0].astype(f32)
        + along_z * padded_ref[1].astype(f32)
        + around * padded_ref[2].astype(f32)
    ) * (quad * kernel_scale)
    dens_high = dens.astype(bf16)
    dens_ref[:PTS] = dens_high
    dens_ref[PTS:] = (dens - dens_high.astype(f32)).astype(bf16)
    by_sector = dot(dens_ref[...], sum_cols_ref[...])
    density_ref[...] = before_ref[...] + exact_dot(sum_rows_ref[...], by_sector[:PTS] + by_sector[PTS:])
    if row_refs:
        copy_rows(mer_ref, nodes_ref, lambda part, at: stress_ref[pl.ds(PTS * part + at, 1), :], row_refs)


def synthesis(section, blk, mer, nodes, blocks, phys, kappa, fwd, table, consts, columns, before):
    forward, backward, sum_rows, sum_cols = consts
    samples = kappa.shape[1]
    last = section == STEPS - 1
    outs = [
        jax.ShapeDtypeStruct((2 * PTS, samples), bf16 if last else f32),
        jax.ShapeDtypeStruct(before.shape, f32),
    ]
    if not last:
        outs += [jax.ShapeDtypeStruct((16, samples), bf16)] * 2
    scratch = [
        pltpu.VMEM((2 * PTS, samples), bf16),
        pltpu.VMEM((4, PTS, samples), bf16),
    ]
    operands = [blk, mer, nodes, *blocks.values(), phys, kappa, fwd, table, forward, backward, columns, sum_rows, sum_cols, before]
    return call(functools.partial(synthesis_kernel, section, tuple(blocks)), "synthesis", outs, operands, 3, scratch, us=3.0)


def merge_kernel(mer_ref, nodes_ref, stress_ref, core_ref, chip_ref, out_ref, total_ref):
    total_ref[...] = stress_ref[...]
    for r_ref, side in zip((core_ref, chip_ref), sides(mer_ref)):
        rows = r_ref[...].astype(f32)
        for part in range(2):
            for k in range(nodes_ref.shape[1]):
                at = 8 * part + k
                total_ref[pl.ds(PTS * part + nodes_ref[side, k], 1), :] += rows[at : at + 1]
    out_ref[...] = total_ref[...].astype(bf16)


def merge(mer, nodes, stress, core, chip):
    shape = jax.ShapeDtypeStruct(stress.shape, bf16)
    scratch = [pltpu.VMEM(stress.shape, f32)]
    return call(merge_kernel, "merge", shape, [mer, nodes, stress, core, chip], 2, scratch, us=0.8)


def analysis_kernel(bits, piece, blk_ref, stress_ref, table_ref, o_ref):
    count = o_ref.shape[2]
    start = block_start(blk_ref, bits, MAXO // len(PARTNERS))
    start = pl.multiple_of(start + piece * count, count)
    order = (lax.broadcasted_iota(jnp.int32, (1, count), 1) + start).astype(f32)
    cosine = dot_t(stress_ref[...], table_ref[0, pl.ds(start, count), :])
    sine = dot_t(stress_ref[...], table_ref[1, pl.ds(start, count), :])
    o_ref[0] = (cosine[:PTS] - order * sine[PTS:]).astype(bf16)
    o_ref[1] = (sine[:PTS] + order * cosine[PTS:]).astype(bf16)


def analysis(bits, piece, blk, stress, table, count, us=0.75):
    shape = jax.ShapeDtypeStruct((2, PTS, count), bf16)
    kernel = functools.partial(analysis_kernel, bits, piece)
    return call(kernel, "analysis", shape, [blk, stress, table], 1, us=us)


def next_values(c, cols, total, parts, now, prev, column_ref, first_order):
    order = lax.broadcasted_iota(jnp.int32, now.shape, 1) + (first_order + cols.start)
    level = column_ref[:, 2:3]
    scale = column_ref[:, 3:4]
    gain = jnp.where(order == 0, scale * (0.5 if c == 0 else 0.0), scale)
    gain = jnp.where(order.astype(f32) < level, gain, 0.0)
    force = sum(p.astype(f32) for p in parts)
    return 2.0 * now - prev - gain * force


def update_kernel(piece, blk_ref, a_ref, b_ref, c_ref, d_ref, now_ref, prev_ref, column_ref, next_ref, send_ref):
    total, width = now_ref.shape[2], next_ref.shape[2]
    cols = slice(piece * width, (piece + 1) * width)
    for c in range(2):
        parts = [p[c] for p in (a_ref, b_ref, c_ref, d_ref)]
        now, prev = now_ref[c, :, cols], prev_ref[c, :, cols]
        value = next_values(c, cols, total, parts, now, prev, column_ref, blk_ref[0, 0] * total)
        next_ref[c] = value
        send_ref[c] = value.astype(bf16)


def update(piece, blk, parts, now, prev, columns):
    outs = [jax.ShapeDtypeStruct(parts[0].shape, f32), jax.ShapeDtypeStruct(parts[0].shape, bf16)]
    kernel = functools.partial(update_kernel, piece)
    return call(kernel, "update", outs, [blk, *parts, now, prev, columns], 1, us=0.3)


def shared_kernel(mer_ref, nodes_ref, a_ref, b_ref, c_ref, d_ref, total_ref, core_ref, chip_ref):
    for c in range(2):
        total_ref[c] = sum(p[c].astype(f32) for p in (a_ref, b_ref, c_ref, d_ref))
    copy_rows(mer_ref, nodes_ref, lambda c, at: total_ref[c, pl.ds(at, 1), :], (core_ref, chip_ref))


def shared(mer, nodes, parts):
    rows = jax.ShapeDtypeStruct((16, parts[0].shape[2]), f32)
    outs = [jax.ShapeDtypeStruct(parts[0].shape, f32), rows, rows]
    return call(shared_kernel, "shared", outs, [mer, nodes, *parts], 2, us=0.5)


def finish_kernel(blk_ref, mer_ref, nodes_ref, force_ref, core_ref, chip_ref, *refs):
    *now_refs, prev_ref, column_ref, out_ref, total_ref = refs
    total_ref[...] = force_ref[...]
    for r_ref, side in zip((core_ref, chip_ref), sides(mer_ref)):
        rows = r_ref[...]
        for c in range(2):
            for k in range(nodes_ref.shape[1]):
                at = 8 * c + k
                total_ref[c, pl.ds(nodes_ref[side, k], 1), :] += rows[at : at + 1]
    points, _, total = out_ref.shape
    width = now_refs[0].shape[2]
    for i, now_ref in enumerate(now_refs):
        cols = slice(i * width, (i + 1) * width)
        for c in range(2):
            force, prev = total_ref[c, :, cols], prev_ref[c, :, cols]
            value = next_values(c, cols, total, [force], now_ref[c], prev, column_ref, blk_ref[0, 0] * total)
            out_ref[:, c, cols] = value[:points]


def finish(blk, mer, nodes, force, core, chip, now, prev, columns, points):
    shape = jax.ShapeDtypeStruct((points, 2, force.shape[2]), f32)
    operands = [blk, mer, nodes, force, core, chip, *now, prev, columns]
    return call(finish_kernel, "finish", shape, operands, 3, [pltpu.VMEM(force.shape, f32)], us=1.3)


def join_kernel(*refs):
    rows = refs[0].shape[0]
    for i, ref in enumerate(refs[:-1]):
        refs[-1][i * rows : (i + 1) * rows] = ref[...]


def everywhere(x, piece):
    return {(bits, piece): swapped(x, "blk", bits) if bits else x for bits in PARTNERS}


def join(*pieces):
    shape = jax.ShapeDtypeStruct((len(pieces) * pieces[0].shape[0], pieces[0].shape[1]), f32)
    return call(join_kernel, "join", shape, pieces, us=0.35)


def joined(x, *bits):
    return join(x, *[swapped(x, "mer", b) for b in bits])


def owners_kernel(first_ref, rows_ref, before_ref, out_ref):
    regions = out_ref.shape[0]
    rows = rows_ref[...]
    count = rows.shape[0]
    names = rows[:, :128].reshape(count // ELEM_ROWS, ELEM_ROWS, 128)
    names = jnp.broadcast_to(names[:, ID_ROW : ID_ROW + 1], names.shape)
    element = lax.broadcasted_iota(jnp.int32, names.shape, 1)
    lane = lax.broadcasted_iota(jnp.int32, names.shape, 2)
    ids = jnp.sum(jnp.where((lane == element) & (element < ID_ROW), names, 0.0), axis=2, keepdims=True)
    ids = jnp.where(element[:, :, :1] < ID_ROW, ids, -1.0).reshape(count, 1)
    mine = (lax.broadcasted_iota(jnp.int32, (count, regions), 1) + first_ref[0, 0]).astype(f32)
    out_ref[...] = before_ref[...] + lax.dot_general(
        jnp.where(ids == mine, 1.0, 0.0),
        rows,
        (((0,), (0,)), ((), ())),
        preferred_element_type=f32,
        precision=lax.Precision.HIGHEST,
    )


def owners(first, rows, before):
    shape = jax.ShapeDtypeStruct(before.shape, f32)
    return call(owners_kernel, "owners", shape, [first, rows, before], 1, us=0.8)


def swapped(x, axis, bits):
    return lax.ppermute(x, axis, [(i, i ^ bits) for i in range(lax.axis_size(axis))])


def across_chips(x):
    ends = range(1, lax.axis_size("mer") - 1)
    return lax.ppermute(x, "mer", [(i, i + 1 if i % 2 else i - 1) for i in ends])


def tied(x, other):
    return lax.optimization_barrier((x, other))[0]


def local(disp_now, disp_prev, kappa, radius, fwd_strain, order_bucket, shared_nodes, region_map):
    points, _, count = disp_now.shape
    elements = order_bucket.shape[0]
    samp_count = kappa.shape[1]
    nphi = 2 * MAXO
    sectors = samp_count // 4
    regions = 4096 // lax.axis_size("mer")
    blk_index = lax.axis_index("blk").astype(jnp.int32)
    blk = blk_index.reshape(1, 1)
    mer = lax.axis_index("mer").astype(jnp.int32).reshape(1, 1)
    first = (lax.axis_index("mer").astype(jnp.int32) * regions).reshape(1, 1)
    buckets = order_bucket.reshape(1, -1)
    nodes = shared_nodes[0]
    in_hbm = lambda x: pltpu.with_memory_space_constraint(x, pltpu.HBM)
    buckets, disp_now, disp_prev = in_hbm(buckets), in_hbm(disp_now), in_hbm(disp_prev)
    current, send = arrange(blk, buckets, disp_now, 1)
    (previous,) = arrange(blk, buckets, disp_prev, 0)
    _, gllw = gll_tables()
    weight = jnp.asarray(np.tile(gllw, elements).reshape(-1, 1), f32)
    columns, density = setup(
        buckets, in_hbm(region_map.reshape(1, -1)), in_hbm(radius.reshape(1, -1)), in_hbm(weight), sectors
    )
    forward, backward = derivative_matrices(elements)
    sum_rows = np.zeros((ELEM_ROWS, PTS), np.float32)
    for e in range(elements):
        sum_rows[e, 25 * e : 25 * e + 25] = 1.0
    sum_cols = np.kron(np.eye(sectors), np.ones((4, 1))).astype(bf16)
    consts = tuple(jnp.asarray(x) for x in (forward, backward, sum_rows, sum_cols))
    blocks = everywhere(send, 0)
    fwd, columns, density, table_blk = lax.optimization_barrier((fwd_strain, columns, density, blk))
    table = fourier_table(table_blk, samp_count)

    late = {place: blocks.pop(place) for place in ((1, 0), (3, 0))}
    phys = tied(early(blk, blocks, table), previous)
    stress, density, core, chip = synthesis(
        0, blk, mer, nodes, late, phys, kappa, fwd, table, consts, columns, density
    )
    chip, core = across_chips(chip), swapped(core, "mer", 1)
    stress = merge(mer, nodes, stress, core, chip)
    pieces = range(PIECES)
    forces = [
        {bits: analysis(bits, h, blk, stress, table, count // len(pieces), us=0.05) for bits in (2, 1, 3, 0)}
        for h in pieces
    ]
    middle, blocks = [], []
    for h in pieces:
        sent = [forces[h][bits] for bits in PARTNERS]
        parts = [swapped(x, "blk", bits) if bits else x for x, bits in zip(sent, PARTNERS)]
        following, send = update(h, blk, parts, current, previous, columns)
        middle.append(following)
        blocks.append(everywhere(send, h))

    stress, density = synthesis(
        1, blk, mer, nodes, blocks[1], early(blk, blocks[0], table), kappa, fwd, table, consts, columns, density
    )
    gathered = swapped(density, "mer", 8)
    forces = {bits: analysis(bits, 0, blk, stress, table, count) for bits in (2, 1)}
    gathered = join(tied(density, forces[2]), gathered)
    forces[3] = analysis(3, 0, blk, tied(stress, gathered), table, count)
    gathered = joined(tied(gathered, [forces[1], forces[3]]), 56)
    forces[0] = analysis(0, 0, blk, stress, table, count)
    parts = [swapped(forces[bits], "blk", bits) if bits else forces[0] for bits in PARTNERS]
    gathered = joined(tied(gathered, [parts[1], forces[0]]), 16)
    force, core, chip = shared(mer, nodes, parts)
    chip, core = across_chips(chip), swapped(core, "mer", 1)
    gathered = tied(gathered, force)
    near = [swapped(gathered, "mer", bits) for bits in (4, 2)]
    gathered = join(gathered, *near, swapped(tied(gathered, [chip, core]), "mer", 6))
    displacement = finish(blk, mer, nodes, force, core, chip, middle, current, columns, points)
    kernel = owners(first, gathered, jnp.zeros((regions, sectors), f32))
    return (displacement, owners(first, swapped(gathered, "mer", 1), kernel))


def solution(mesh):
    in_specs = (
        P("mer", None, "blk"),
        P("mer", None, "blk"),
        P("mer", "blk"),
        P("mer"),
        P(None, None, "mer", "blk"),
        P("mer"),
        P("mer", None, None),
        P("mer"),
    )
    out_specs = (P("mer", None, "blk"), P("mer", "blk"))
    return jax.shard_map(local, mesh=mesh, in_specs=in_specs, out_specs=out_specs, check_vma=False)
```

```python
import functools
import math

import jax
import jax.numpy as jnp
import numpy as np
from jax import lax
from jax.experimental import pallas as pl
from jax.experimental.pallas import tpu as pltpu
from jax.sharding import PartitionSpec as P

MAXO = 2048
STEPS = 2
PIECES = 2
PTS = 128
ELEM_ROWS = 8
ID_ROW = 5
TABLE_STRIDE = 64
FLOPS_US = 3450000000
PARTNERS = (0, 2, 1, 3)

time_step_sq = 0.0004
kernel_scale = 0.0001
bucket_orders = (8, 64, 512, 2048)

f32 = jnp.float32
bf16 = jnp.bfloat16


def gll_tables():
    nodes = np.array([-1.0, -math.sqrt(3.0 / 7.0), 0.0, math.sqrt(3.0 / 7.0), 1.0])
    weights_line = np.array([0.1, 49.0 / 90.0, 32.0 / 45.0, 49.0 / 90.0, 0.1])
    legendre = (35.0 * nodes**4 - 30.0 * nodes**2 + 3.0) / 8.0
    deriv = np.zeros((5, 5))
    for row_index in range(5):
        for col_index in range(5):
            if row_index != col_index:
                deriv[row_index, col_index] = (
                    legendre[row_index]
                    / legendre[col_index]
                    / (nodes[row_index] - nodes[col_index])
                )
    deriv[0, 0] = -5.0
    deriv[4, 4] = 5.0
    return (deriv, np.outer(weights_line, weights_line).reshape(25))


def split_const(x):
    high = np.asarray(x, np.float32).astype(bf16)
    low = (np.asarray(x, np.float32) - high.astype(np.float32)).astype(bf16)
    return high, low


def derivative_matrices(elements):
    deriv, _ = gll_tables()
    along_s = np.zeros((PTS, PTS))
    along_z = np.zeros((PTS, PTS))
    for e in range(elements):
        base = slice(25 * e, 25 * e + 25)
        along_s[base, base] = np.kron(deriv, np.eye(5))
        along_z[base, base] = np.kron(np.eye(5), deriv)
    both = np.concatenate([along_s, along_z])
    high, low = split_const(both)
    forward = np.concatenate([high, high, low], axis=1)
    high_t, low_t = split_const(both.T)
    return forward, np.concatenate([high_t, low_t], axis=1)


def small_tables(samples):
    coarse = TABLE_STRIDE * np.arange(MAXO // TABLE_STRIDE)
    every = np.concatenate([coarse, np.arange(TABLE_STRIDE)])
    angle = (every[:, None] * np.arange(samples)[None, :] % (2 * MAXO)) * (math.pi / MAXO)
    return np.stack([np.cos(angle), np.sin(angle)]).astype(np.float32)


def table_kernel(blk_ref, small_ref, out_ref, fine_ref):
    coarse = MAXO // TABLE_STRIDE
    quarters = lax.broadcasted_iota(jnp.int32, (TABLE_STRIDE, 1), 0) * blk_ref[0, 0]
    quarters = jnp.bitwise_and(quarters, 3)
    by_cos = jnp.where(quarters == 0, 1.0, jnp.where(quarters == 2, -1.0, 0.0))
    by_sin = jnp.where(quarters == 1, 1.0, jnp.where(quarters == 3, -1.0, 0.0))
    fine_cos, fine_sin = small_ref[0, coarse:, :], small_ref[1, coarse:, :]
    fine_ref[0] = fine_cos * by_cos - fine_sin * by_sin
    fine_ref[1] = fine_sin * by_cos + fine_cos * by_sin

    def one(a, carry):
        big_cos = small_ref[0, pl.ds(a, 1), :]
        big_sin = small_ref[1, pl.ds(a, 1), :]
        start = pl.multiple_of(a * TABLE_STRIDE, TABLE_STRIDE)
        for part in range(0, TABLE_STRIDE, 16):
            fine_cos = fine_ref[0, part : part + 16, :]
            fine_sin = fine_ref[1, part : part + 16, :]
            rows = pl.ds(pl.multiple_of(start + part, 16), 16)
            out_ref[0, rows, :] = (big_cos * fine_cos - big_sin * fine_sin).astype(bf16)
            out_ref[1, rows, :] = (big_sin * fine_cos + big_cos * fine_sin).astype(bf16)
        return carry

    lax.fori_loop(0, coarse, one, 0)


VMEM = pl.BlockSpec(memory_space=pltpu.VMEM)
SMEM = pl.BlockSpec(memory_space=pltpu.SMEM)


def call(kernel, name, out_shape, operands, scalars=0, scratch=(), us=1.0):
    single = not isinstance(out_shape, (list, tuple))
    return pl.pallas_call(
        kernel,
        in_specs=[SMEM] * scalars + [VMEM] * (len(operands) - scalars),
        out_specs=VMEM if single else [VMEM] * len(out_shape),
        out_shape=out_shape,
        scratch_shapes=list(scratch),
        name=name,
        compiler_params=pltpu.CompilerParams(vmem_limit_bytes=16 * 1024 * 1024),
        cost_estimate=pl.CostEstimate(flops=int(us * FLOPS_US), bytes_accessed=0, transcendentals=0),
    )(*operands)


def block_start(blk_ref, bits, count):
    blk = blk_ref[0, 0]
    partner = (blk, blk + 1 - 2 * lax.rem(blk, 2), lax.rem(blk + 2, 4), 3 - blk)[bits]
    return pl.multiple_of(partner * count, count)


def fourier_table(blk, samples):
    shape = jax.ShapeDtypeStruct((2, MAXO, samples), bf16)
    small = jnp.asarray(small_tables(samples))
    return call(table_kernel, "table", shape, [blk, small], 1, [pltpu.VMEM((2, TABLE_STRIDE, samples), f32)])


def dot(a, b):
    return jnp.dot(a, b, preferred_element_type=f32)


def dot_t(a, b):
    return lax.dot_general(a, b, (((1,), (1,)), ((), ())), preferred_element_type=f32)


def exact_dot(a, b):
    return jnp.dot(a, b, preferred_element_type=f32, precision=lax.Precision.HIGHEST)


def levels_of(bucket_ref, points):
    point = lax.broadcasted_iota(jnp.int32, (points, 1), 0)
    level = jnp.zeros((points, 1), jnp.int32)
    for e in range(bucket_ref.shape[1]):
        value = jnp.int32(0)
        for position, orders in enumerate(bucket_orders):
            value = jnp.where(bucket_ref[0, e] == position, orders, value)
        level = jnp.where((point >= 25 * e) & (point < 25 * e + 25), value, level)
    return level


def arrange_kernel(blk_ref, bucket_hbm, disp_hbm, now_ref, *rest):
    *send_ref, disp_ref, bucket_ref, sems = rest
    points, _, count = disp_ref.shape
    buckets = pltpu.make_async_copy(bucket_hbm, bucket_ref, sems.at[0])
    field = pltpu.make_async_copy(disp_hbm, disp_ref, sems.at[1])
    buckets.start()
    field.start()
    now_ref[:, points:, :] = jnp.zeros((2, now_ref.shape[1] - points, count), f32)
    buckets.wait()
    order = lax.broadcasted_iota(jnp.int32, (points, count), 1) + blk_ref[0, 0] * count
    inside = order < levels_of(bucket_ref, points)
    field.wait()
    for c in range(2):
        kept = inside if c == 0 else inside & (order >= 1)
        now_ref[c, :points, :] = jnp.where(kept, disp_ref[:, c, :], 0.0)
    for i, s_ref in enumerate(send_ref):
        width = s_ref.shape[2]
        s_ref[...] = now_ref[:, :, i * width : (i + 1) * width].astype(bf16)


def arrange(blk, buckets, disp, pieces):
    shape = (2, PTS, disp.shape[2])
    sent = [jax.ShapeDtypeStruct((2, PTS, disp.shape[2] // pieces), bf16)] * pieces if pieces else []
    hbm = pl.BlockSpec(memory_space=pltpu.HBM)
    return pl.pallas_call(
        arrange_kernel,
        in_specs=[SMEM, hbm, hbm],
        out_specs=[VMEM] * (1 + pieces),
        out_shape=[jax.ShapeDtypeStruct(shape, f32), *sent],
        scratch_shapes=[
            pltpu.VMEM(disp.shape, f32),
            pltpu.SMEM(buckets.shape, jnp.int32),
            pltpu.SemaphoreType.DMA((2,)),
        ],
        name="arrange",
        compiler_params=pltpu.CompilerParams(vmem_limit_bytes=16 * 1024 * 1024),
    )(blk, buckets, disp)


def setup_kernel(bucket_ref, region_ref, radius_ref, weight_ref, column_ref, density_ref):
    points = radius_ref.shape[1]
    square = (points, points)
    diagonal = lax.broadcasted_iota(jnp.int32, square, 0) == lax.broadcasted_iota(jnp.int32, square, 1)
    radius = jnp.sum(jnp.where(diagonal, radius_ref[...], 0.0), axis=1, keepdims=True)
    weight = weight_ref[...] * radius
    column_ref[...] = jnp.zeros(column_ref.shape, f32)
    column_ref[:points, 0:1] = 1.0 / radius
    column_ref[:points, 1:2] = weight * (2.0 * math.pi / (2 * MAXO))
    column_ref[:points, 2:3] = levels_of(bucket_ref, points).astype(f32)
    column_ref[:points, 3:4] = time_step_sq / (weight * math.pi)
    shape = density_ref.shape
    row, lane = lax.broadcasted_iota(jnp.int32, shape, 0), lax.broadcasted_iota(jnp.int32, shape, 1)
    density = jnp.zeros(shape, f32)
    for e in range(region_ref.shape[1]):
        name = region_ref[0, e].astype(f32)
        density = jnp.where((row == ID_ROW) & (lane == e), name, density)
    density_ref[...] = density


def setup(buckets, regions, radius, weight, sectors):
    outs = [jax.ShapeDtypeStruct((PTS, 4), f32), jax.ShapeDtypeStruct((ELEM_ROWS, sectors), f32)]
    return call(setup_kernel, "setup", outs, [buckets, regions, radius, weight], 2)


def sides(mer_ref):
    here = 1 - lax.rem(mer_ref[0, 0], 2)
    return here, 1 - here


def coefficients_times_table(blk_ref, places, block_refs, table_ref):
    total = 0.0
    for (bits, piece), u_ref in zip(places, block_refs, strict=True):
        count = u_ref.shape[2]
        start = block_start(blk_ref, bits, MAXO // len(PARTNERS))
        start = pl.multiple_of(start + piece * count, count)
        order = (lax.broadcasted_iota(jnp.int32, (1, count), 1) + start).astype(f32)
        u0, u1 = u_ref[0], u_ref[1]
        cosine = jnp.concatenate([u0, (order * u1.astype(f32)).astype(bf16)])
        sine = jnp.concatenate([u1, (-order * u0.astype(f32)).astype(bf16)])
        total += dot(cosine, table_ref[0, pl.ds(start, count), :])
        total += dot(sine, table_ref[1, pl.ds(start, count), :])
    return total


def copy_rows(mer_ref, nodes_ref, row, out_refs):
    for o_ref, side in zip(out_refs, sides(mer_ref)):
        rows = []
        for part in range(2):
            rows += [row(part, nodes_ref[side, k]) for k in range(nodes_ref.shape[1])]
            rows.append(jnp.zeros((8 - nodes_ref.shape[1], o_ref.shape[1]), f32))
        o_ref[...] = jnp.concatenate(rows).astype(o_ref.dtype)


def early_kernel(places, blk_ref, *refs):
    *block_refs, table_ref, phys_ref = refs
    phys_ref[...] = coefficients_times_table(blk_ref, places, block_refs, table_ref)


def early(blk, blocks, table):
    shape = jax.ShapeDtypeStruct((2 * PTS, table.shape[2]), f32)
    kernel = functools.partial(early_kernel, tuple(blocks))
    return call(kernel, "early", shape, [blk, *blocks.values(), table], 1, us=1.3)


def synthesis_kernel(section, places, blk_ref, mer_ref, nodes_ref, *refs):
    block_refs = refs[: len(places)]
    (
        phys_ref,
        kappa_ref,
        fwd_ref,
        table_ref,
        forward_ref,
        backward_ref,
        column_ref,
        sum_rows_ref,
        sum_cols_ref,
        before_ref,
        stress_ref,
        density_ref,
        *row_refs,
        dens_ref,
        padded_ref,
    ) = refs[len(places) :]
    points, samples = kappa_ref.shape
    inv_radius = column_ref[:, 0:1]
    quad = column_ref[:, 1:2]
    for i in range(4):
        padded_ref[i, PTS - 16 :, :] = jnp.zeros((16, samples), bf16)
        padded_ref[i, :points, :] = fwd_ref[section, i] if i < 3 else kappa_ref[...]
    phys = phys_ref[...] + coefficients_times_table(blk_ref, places, block_refs, table_ref)
    field, around = phys[:PTS], phys[PTS:] * inv_radius
    high = field.astype(bf16)
    low = (field - high.astype(f32)).astype(bf16)
    along = dot(forward_ref[...], jnp.concatenate([high, low, high]))
    along_s, along_z = along[:PTS], along[PTS:]
    modulus = padded_ref[3].astype(f32) * quad
    stress = jnp.concatenate([along_s * modulus, along_z * modulus]).astype(bf16)
    stress_ref[:PTS] = dot(backward_ref[...], jnp.concatenate([stress, stress])).astype(stress_ref.dtype)
    stress_ref[PTS:] = (around * modulus * inv_radius).astype(stress_ref.dtype)
    dens = (
        along_s * padded_ref[0].astype(f32)
        + along_z * padded_ref[1].astype(f32)
        + around * padded_ref[2].astype(f32)
    ) * (quad * kernel_scale)
    dens_high = dens.astype(bf16)
    dens_ref[:PTS] = dens_high
    dens_ref[PTS:] = (dens - dens_high.astype(f32)).astype(bf16)
    by_sector = dot(dens_ref[...], sum_cols_ref[...])
    density_ref[...] = before_ref[...] + exact_dot(sum_rows_ref[...], by_sector[:PTS] + by_sector[PTS:])
    if row_refs:
        copy_rows(mer_ref, nodes_ref, lambda part, at: stress_ref[pl.ds(PTS * part + at, 1), :], row_refs)


def synthesis(section, blk, mer, nodes, blocks, phys, kappa, fwd, table, consts, columns, before):
    forward, backward, sum_rows, sum_cols = consts
    samples = kappa.shape[1]
    last = section == STEPS - 1
    outs = [
        jax.ShapeDtypeStruct((2 * PTS, samples), bf16 if last else f32),
        jax.ShapeDtypeStruct(before.shape, f32),
    ]
    if not last:
        outs += [jax.ShapeDtypeStruct((16, samples), bf16)] * 2
    scratch = [
        pltpu.VMEM((2 * PTS, samples), bf16),
        pltpu.VMEM((4, PTS, samples), bf16),
    ]
    operands = [blk, mer, nodes, *blocks.values(), phys, kappa, fwd, table, forward, backward, columns, sum_rows, sum_cols, before]
    return call(functools.partial(synthesis_kernel, section, tuple(blocks)), "synthesis", outs, operands, 3, scratch, us=3.0)


def merge_kernel(mer_ref, nodes_ref, stress_ref, core_ref, chip_ref, out_ref, total_ref):
    total_ref[...] = stress_ref[...]
    for r_ref, side in zip((core_ref, chip_ref), sides(mer_ref)):
        rows = r_ref[...].astype(f32)
        for part in range(2):
            for k in range(nodes_ref.shape[1]):
                at = 8 * part + k
                total_ref[pl.ds(PTS * part + nodes_ref[side, k], 1), :] += rows[at : at + 1]
    out_ref[...] = total_ref[...].astype(bf16)


def merge(mer, nodes, stress, core, chip):
    shape = jax.ShapeDtypeStruct(stress.shape, bf16)
    scratch = [pltpu.VMEM(stress.shape, f32)]
    return call(merge_kernel, "merge", shape, [mer, nodes, stress, core, chip], 2, scratch, us=0.8)


def analysis_kernel(bits, piece, blk_ref, stress_ref, table_ref, o_ref):
    count = o_ref.shape[2]
    start = block_start(blk_ref, bits, MAXO // len(PARTNERS))
    start = pl.multiple_of(start + piece * count, count)
    order = (lax.broadcasted_iota(jnp.int32, (1, count), 1) + start).astype(f32)
    cosine = dot_t(stress_ref[...], table_ref[0, pl.ds(start, count), :])
    sine = dot_t(stress_ref[...], table_ref[1, pl.ds(start, count), :])
    o_ref[0] = (cosine[:PTS] - order * sine[PTS:]).astype(bf16)
    o_ref[1] = (sine[:PTS] + order * cosine[PTS:]).astype(bf16)


def analysis(bits, piece, blk, stress, table, count, us=0.75):
    shape = jax.ShapeDtypeStruct((2, PTS, count), bf16)
    kernel = functools.partial(analysis_kernel, bits, piece)
    return call(kernel, "analysis", shape, [blk, stress, table], 1, us=us)


def next_values(c, cols, total, parts, now, prev, column_ref, first_order):
    order = lax.broadcasted_iota(jnp.int32, now.shape, 1) + (first_order + cols.start)
    level = column_ref[:, 2:3]
    scale = column_ref[:, 3:4]
    gain = jnp.where(order == 0, scale * (0.5 if c == 0 else 0.0), scale)
    gain = jnp.where(order.astype(f32) < level, gain, 0.0)
    force = sum(p.astype(f32) for p in parts)
    return 2.0 * now - prev - gain * force


def update_kernel(piece, blk_ref, a_ref, b_ref, c_ref, d_ref, now_ref, prev_ref, column_ref, next_ref, send_ref):
    total, width = now_ref.shape[2], next_ref.shape[2]
    cols = slice(piece * width, (piece + 1) * width)
    for c in range(2):
        parts = [p[c] for p in (a_ref, b_ref, c_ref, d_ref)]
        now, prev = now_ref[c, :, cols], prev_ref[c, :, cols]
        value = next_values(c, cols, total, parts, now, prev, column_ref, blk_ref[0, 0] * total)
        next_ref[c] = value
        send_ref[c] = value.astype(bf16)


def update(piece, blk, parts, now, prev, columns):
    outs = [jax.ShapeDtypeStruct(parts[0].shape, f32), jax.ShapeDtypeStruct(parts[0].shape, bf16)]
    kernel = functools.partial(update_kernel, piece)
    return call(kernel, "update", outs, [blk, *parts, now, prev, columns], 1, us=0.3)


def shared_kernel(mer_ref, nodes_ref, a_ref, b_ref, c_ref, d_ref, total_ref, core_ref, chip_ref):
    for c in range(2):
        total_ref[c] = sum(p[c].astype(f32) for p in (a_ref, b_ref, c_ref, d_ref))
    copy_rows(mer_ref, nodes_ref, lambda c, at: total_ref[c, pl.ds(at, 1), :], (core_ref, chip_ref))


def shared(mer, nodes, parts):
    rows = jax.ShapeDtypeStruct((16, parts[0].shape[2]), bf16)
    outs = [jax.ShapeDtypeStruct(parts[0].shape, f32), rows, rows]
    return call(shared_kernel, "shared", outs, [mer, nodes, *parts], 2, us=0.5)


def finish_kernel(blk_ref, mer_ref, nodes_ref, force_ref, core_ref, chip_ref, *refs):
    *now_refs, prev_ref, column_ref, out_ref, total_ref = refs
    total_ref[...] = force_ref[...]
    for r_ref, side in zip((core_ref, chip_ref), sides(mer_ref)):
        rows = r_ref[...].astype(f32)
        for c in range(2):
            for k in range(nodes_ref.shape[1]):
                at = 8 * c + k
                total_ref[c, pl.ds(nodes_ref[side, k], 1), :] += rows[at : at + 1]
    points, _, total = out_ref.shape
    width = now_refs[0].shape[2]
    for i, now_ref in enumerate(now_refs):
        cols = slice(i * width, (i + 1) * width)
        for c in range(2):
            force, prev = total_ref[c, :, cols], prev_ref[c, :, cols]
            value = next_values(c, cols, total, [force], now_ref[c], prev, column_ref, blk_ref[0, 0] * total)
            out_ref[:, c, cols] = value[:points]


def finish(blk, mer, nodes, force, core, chip, now, prev, columns, points):
    shape = jax.ShapeDtypeStruct((points, 2, force.shape[2]), f32)
    operands = [blk, mer, nodes, force, core, chip, *now, prev, columns]
    return call(finish_kernel, "finish", shape, operands, 3, [pltpu.VMEM(force.shape, f32)], us=1.3)


def join_kernel(*refs):
    rows = refs[0].shape[0]
    for i, ref in enumerate(refs[:-1]):
        refs[-1][i * rows : (i + 1) * rows] = ref[...]


def everywhere(x, piece):
    return {(bits, piece): swapped(x, "blk", bits) if bits else x for bits in PARTNERS}


def join(*pieces):
    shape = jax.ShapeDtypeStruct((len(pieces) * pieces[0].shape[0], pieces[0].shape[1]), f32)
    return call(join_kernel, "join", shape, pieces, us=0.35)


def joined(x, *bits):
    return join(x, *[swapped(x, "mer", b) for b in bits])


def owners_kernel(first_ref, rows_ref, before_ref, out_ref):
    regions = out_ref.shape[0]
    rows = rows_ref[...]
    count = rows.shape[0]
    names = rows[:, :128].reshape(count // ELEM_ROWS, ELEM_ROWS, 128)
    names = jnp.broadcast_to(names[:, ID_ROW : ID_ROW + 1], names.shape)
    element = lax.broadcasted_iota(jnp.int32, names.shape, 1)
    lane = lax.broadcasted_iota(jnp.int32, names.shape, 2)
    ids = jnp.sum(jnp.where((lane == element) & (element < ID_ROW), names, 0.0), axis=2, keepdims=True)
    ids = jnp.where(element[:, :, :1] < ID_ROW, ids, -1.0).reshape(count, 1)
    mine = (lax.broadcasted_iota(jnp.int32, (count, regions), 1) + first_ref[0, 0]).astype(f32)
    out_ref[...] = before_ref[...] + lax.dot_general(
        jnp.where(ids == mine, 1.0, 0.0),
        rows,
        (((0,), (0,)), ((), ())),
        preferred_element_type=f32,
        precision=lax.Precision.HIGHEST,
    )


def owners(first, rows, before):
    shape = jax.ShapeDtypeStruct(before.shape, f32)
    return call(owners_kernel, "owners", shape, [first, rows, before], 1, us=0.8)


def swapped(x, axis, bits):
    return lax.ppermute(x, axis, [(i, i ^ bits) for i in range(lax.axis_size(axis))])


def across_chips(x):
    ends = range(1, lax.axis_size("mer") - 1)
    return lax.ppermute(x, "mer", [(i, i + 1 if i % 2 else i - 1) for i in ends])


def tied(x, other):
    return lax.optimization_barrier((x, other))[0]


def local(disp_now, disp_prev, kappa, radius, fwd_strain, order_bucket, shared_nodes, region_map):
    points, _, count = disp_now.shape
    elements = order_bucket.shape[0]
    samp_count = kappa.shape[1]
    nphi = 2 * MAXO
    sectors = samp_count // 4
    regions = 4096 // lax.axis_size("mer")
    blk_index = lax.axis_index("blk").astype(jnp.int32)
    blk = blk_index.reshape(1, 1)
    mer = lax.axis_index("mer").astype(jnp.int32).reshape(1, 1)
    first = (lax.axis_index("mer").astype(jnp.int32) * regions).reshape(1, 1)
    buckets = order_bucket.reshape(1, -1)
    nodes = shared_nodes[0]
    in_hbm = lambda x: pltpu.with_memory_space_constraint(x, pltpu.HBM)
    buckets, disp_now, disp_prev = in_hbm(buckets), in_hbm(disp_now), in_hbm(disp_prev)
    current, send = arrange(blk, buckets, disp_now, 1)
    (previous,) = arrange(blk, buckets, disp_prev, 0)
    _, gllw = gll_tables()
    weight = jnp.asarray(np.tile(gllw, elements).reshape(-1, 1), f32)
    columns, density = setup(
        buckets, in_hbm(region_map.reshape(1, -1)), in_hbm(radius.reshape(1, -1)), in_hbm(weight), sectors
    )
    forward, backward = derivative_matrices(elements)
    sum_rows = np.zeros((ELEM_ROWS, PTS), np.float32)
    for e in range(elements):
        sum_rows[e, 25 * e : 25 * e + 25] = 1.0
    sum_cols = np.kron(np.eye(sectors), np.ones((4, 1))).astype(bf16)
    consts = tuple(jnp.asarray(x) for x in (forward, backward, sum_rows, sum_cols))
    blocks = everywhere(send, 0)
    fwd, columns, density, table_blk = lax.optimization_barrier((fwd_strain, columns, density, blk))
    table = fourier_table(table_blk, samp_count)

    late = {place: blocks.pop(place) for place in ((1, 0), (3, 0))}
    phys = tied(early(blk, blocks, table), previous)
    stress, density, core, chip = synthesis(
        0, blk, mer, nodes, late, phys, kappa, fwd, table, consts, columns, density
    )
    chip, core = across_chips(chip), swapped(core, "mer", 1)
    stress = merge(mer, nodes, stress, core, chip)
    pieces = range(PIECES)
    forces = [
        {bits: analysis(bits, h, blk, stress, table, count // len(pieces), us=0.05) for bits in (2, 1, 3, 0)}
        for h in pieces
    ]
    middle, blocks = [], []
    for h in pieces:
        sent = [forces[h][bits] for bits in PARTNERS]
        parts = [swapped(x, "blk", bits) if bits else x for x, bits in zip(sent, PARTNERS)]
        following, send = update(h, blk, parts, current, previous, columns)
        middle.append(following)
        blocks.append(everywhere(send, h))

    stress, density = synthesis(
        1, blk, mer, nodes, blocks[1], early(blk, blocks[0], table), kappa, fwd, table, consts, columns, density
    )
    gathered = swapped(density, "mer", 8)
    forces = {bits: analysis(bits, 0, blk, stress, table, count) for bits in (2, 1)}
    gathered = join(tied(density, forces[2]), gathered)
    forces[3] = analysis(3, 0, blk, tied(stress, gathered), table, count)
    gathered = joined(tied(gathered, [forces[1], forces[3]]), 56)
    forces[0] = analysis(0, 0, blk, stress, table, count)
    parts = [swapped(forces[bits], "blk", bits) if bits else forces[0] for bits in PARTNERS]
    gathered = joined(tied(gathered, [parts[1], forces[0]]), 16)
    force, core, chip = shared(mer, nodes, parts)
    chip, core = across_chips(chip), swapped(core, "mer", 1)
    gathered = tied(gathered, force)
    near = [swapped(gathered, "mer", bits) for bits in (4, 2)]
    gathered = join(gathered, *near, swapped(tied(gathered, [chip, core]), "mer", 6))
    displacement = finish(blk, mer, nodes, force, core, chip, middle, current, columns, points)
    kernel = owners(first, gathered, jnp.zeros((regions, sectors), f32))
    return (displacement, owners(first, swapped(gathered, "mer", 1), kernel))


def solution(mesh):
    in_specs = (
        P("mer", None, "blk"),
        P("mer", None, "blk"),
        P("mer", "blk"),
        P("mer"),
        P(None, None, "mer", "blk"),
        P("mer"),
        P("mer", None, None),
        P("mer"),
    )
    out_specs = (P("mer", None, "blk"), P("mer", "blk"))
    return jax.shard_map(local, mesh=mesh, in_specs=in_specs, out_specs=out_specs, check_vma=False)
```
